256 devices in a mesh: dp: 4 (over y), expert: 64 (over z, x, core).
Axes of the slice: x: 4, y: 4, z: 8, core: 2. Of those that a mesh axis runs over, the one named last changes fastest.
Arguments:
- tokens: bfloat16 [32768, 2048], P(('dp', 'expert')), may hold values from -6 to 6
- cotangent: bfloat16 [32768, 2048], P(('dp', 'expert')), may hold values from -0.3984375 to 0.3984375
- routing: int32 [32768, 8], P(('dp', 'expert')), may hold values from 0 to 31, as said below
- router_route_weights: float32 [32768, 8], P(('dp', 'expert')), may hold values from 0.1 to 1
- route_replica_choice: int32 [32768, 8], P(('dp', 'expert')), may hold values from 0 to 11
- device_expert_table: int32 [64], replicated, may hold values from 0 to 31, as said below
- gate_up_weight: bfloat16 [64, 2048, 1536], P('expert'), may hold values from -1 to 1, as said below
- down_weight: bfloat16 [64, 768, 2048], P('expert'), may hold values from -1 to 1, as said below
- adapter_down_maps: bfloat16 [64, 2048, 128], P('expert'), may hold values from -1 to 1, as said below
- adapter_up_maps: bfloat16 [64, 2, 64, 768], P('expert'), may hold values from -2 to 2, as said below
Outputs:
- mixed: bfloat16 [32768, 2048], P(('dp', 'expert'))
- grad_a: float32 [64, 2048, 128], P('expert')
- grad_b: float32 [64, 2, 64, 768], P('expert')
The draws below stay inside these ranges and needn't reach their ends.
Inputs may be any that keep to these rules, and one draw needn't show every extreme that they name: `routing`: each row names 8 different experts; experts held by more entries of device_expert_table are chosen more often. `device_expert_table`: every expert of 0 to 31 is held by one to four entries. `gate_up_weight`: entries of device_expert_table that are equal hold equal matrices. `down_weight`: entries of device_expert_table that are equal hold equal matrices. `adapter_down_maps`: entries of device_expert_table that are equal hold equal matrices. `adapter_up_maps`: entries of device_expert_table that are equal hold equal matrices.
All inputs are finite; a program needn't handle non-finite values.
Results may differ from the reference program's by a relative error of at most 0.006.
Values may be sent and summed in bfloat16 or wider, within the bound.
A program may use at most 128 MiB of HBM per device.

```python
import math
import jax
import jax.numpy as jnp
from jax import lax

D = 2048
FF = 768
RANK = 64
TOP = 8
TOK_DEV = 128
SLOTS = 64
EXPERTS = 32
CAP = 16
TOKENS = 32768
N_DP = 4


def place_slots(key):
    extra_slots = SLOTS - EXPERTS
    heavy_count = (extra_slots + 7) // 8 if extra_slots >= 3 else 0
    expert_order = jax.random.permutation(jax.random.fold_in(key, 101), EXPERTS)
    chosen = jnp.concatenate([jnp.arange(3 * heavy_count, dtype=jnp.int32) // 3, heavy_count + jnp.arange(extra_slots - 3 * heavy_count, dtype=jnp.int32)])
    entries = jnp.concatenate([jnp.arange(EXPERTS, dtype=jnp.int32), expert_order[chosen].astype(jnp.int32)])
    shuffle = jax.random.permutation(jax.random.fold_in(key, 102), SLOTS)
    return entries[shuffle].astype(jnp.int32)


def expert_copies(placement, inner_key, shape, scale):

    def one_slot(expert_id):
        slot_key = jax.random.fold_in(inner_key, expert_id)
        normal_like = jax.random.normal(jax.random.fold_in(slot_key, 1), shape, jnp.float32)
        normal_like = jnp.clip(normal_like, -4.0, 4.0)
        return scale * normal_like
    return jax.vmap(one_slot)(placement)


def draw_routing(key, part):
    placement = place_slots(key)
    key = jax.random.fold_in(key, 15)
    expert_ids = jnp.arange(EXPERTS, dtype=jnp.int32)
    copies = jnp.sum((expert_ids[:, None] == placement[None, :]).astype(jnp.int32), axis=1)
    noise = jax.random.randint(key, (TOKENS, EXPERTS), 0, 1024, dtype=jnp.int32)
    score = (noise + 160 * (copies[None, :] - 1)) * EXPERTS + expert_ids[None, :]
    values, picked = lax.top_k(score, TOP)
    return picked.astype(jnp.int32)


def draw_device_expert_table(key, part):
    return place_slots(key)


def draw_gate_up_weight(key, part):
    placement = place_slots(key)
    key = jax.random.fold_in(key, 11)
    return expert_copies(placement, key, (D, 2 * FF), D ** (-0.5)).astype(jnp.bfloat16)


def draw_down_weight(key, part):
    placement = place_slots(key)
    key = jax.random.fold_in(key, 12)
    return expert_copies(placement, key, (FF, D), FF ** (-0.5)).astype(jnp.bfloat16)


def draw_adapter_down_maps(key, part):
    placement = place_slots(key)
    key = jax.random.fold_in(key, 13)
    return expert_copies(placement, key, (D, 2 * RANK), D ** (-0.5)).astype(jnp.bfloat16)


def draw_adapter_up_maps(key, part):
    placement = place_slots(key)
    key = jax.random.fold_in(key, 14)
    return expert_copies(placement, key, (2, RANK, FF), RANK ** (-0.5)).astype(jnp.bfloat16)


def set_ends(drawn, key, least, high):
    longest = drawn.shape.index(max(drawn.shape))
    spots = []
    for shift in (0, 1):
        where = [jax.random.randint(jax.random.fold_in(key, axis), (), 0, length) for axis, length in enumerate(drawn.shape)]
        where[longest] = (where[longest] + shift) % drawn.shape[longest]
        spots.append(tuple(where))
    return drawn.at[spots[0]].set(least).at[spots[1]].set(high)


def shard_levels(rng, shape, shards, low, largest):
    factor_of = 1.0
    for dim, shards_of in shards:
        draws = jax.random.uniform(jax.random.fold_in(jax.random.fold_in(rng, 6), dim), (shards_of,), jnp.float32, low / len(shards), largest / len(shards))
        factor_of = factor_of * jnp.repeat(jnp.exp(draws), shape[dim] // shards_of).reshape((-1,) + (1,) * (len(shape) - 1 - dim))
    return factor_of


def bell_draw(own_key, dims, deviation, most, pieces=(), kind=jnp.bfloat16):
    values = jax.random.normal(own_key, dims, jnp.float32) * deviation
    if len(pieces) > 0:
        values = shard_levels(own_key, dims, pieces, -0.22, 0.18) * values
    return jnp.clip(values, min=-most, max=most).astype(kind)


def setup_inputs(seed: int = 0) -> dict:
    key_of = jax.random.split(jax.random.key(seed), 11)
    return {
        "tokens": bell_draw(key_of[0], (TOKENS, D), 1.0, 6.0, ((0, 256),)),
        "cotangent": bell_draw(key_of[1], (TOKENS, D), 0.0625, 0.3984375, ((0, 256),)),
        "routing": draw_routing(jax.random.fold_in(key_of[10], 71), 0),
        "router_route_weights": jnp.clip(jnp.exp(math.log(1.0) - 2.3025851 * jax.random.uniform(key_of[3], (TOKENS, TOP), jnp.float32) ** shard_levels(key_of[3], (TOKENS, TOP), ((0, 256),), -0.2, 0.2)), 0.1, 1.0),
        "route_replica_choice": set_ends(jax.random.randint(key_of[4], (TOKENS, TOP), 0, 12), jax.random.fold_in(key_of[4], 1), 0, 11).astype(jnp.int32),
        "device_expert_table": draw_device_expert_table(jax.random.fold_in(key_of[10], 71), 0),
        "gate_up_weight": draw_gate_up_weight(jax.random.fold_in(key_of[10], 71), 0),
        "down_weight": draw_down_weight(jax.random.fold_in(key_of[10], 71), 0),
        "adapter_down_maps": draw_adapter_down_maps(jax.random.fold_in(key_of[10], 71), 0),
        "adapter_up_maps": draw_adapter_up_maps(jax.random.fold_in(key_of[10], 71), 0),
    }


ADAPTER_SCALE = 0.5


def route_rows(routing, route_replica_choice, device_expert_table, capacity):
    slot_total = device_expert_table.shape[0]
    route_total = routing.shape[0] * routing.shape[1]
    expert_flat = routing.reshape(-1).astype(jnp.int32)
    holds_mask = (expert_flat[:, None] == device_expert_table[None, :]).astype(jnp.int32)
    copies = jnp.sum(holds_mask, axis=1).astype(jnp.int32)
    wanted = (route_replica_choice.reshape(-1).astype(jnp.int32) % copies).astype(jnp.int32)
    before = (jnp.cumsum(holds_mask, axis=1).astype(jnp.int32) - holds_mask).astype(jnp.int32)
    picked = (holds_mask * (before == wanted[:, None]).astype(jnp.int32)).astype(jnp.int32)
    ahead_of = (jnp.cumsum(picked, axis=0).astype(jnp.int32) - picked).astype(jnp.int32)
    position = jnp.sum(picked * ahead_of, axis=1).astype(jnp.int32)
    target = jnp.sum(picked * jnp.arange(slot_total, dtype=jnp.int32)[None, :], axis=1).astype(jnp.int32)
    kept_mask = position < capacity
    dest_index = jnp.where(kept_mask, target * capacity + position, slot_total * capacity).astype(jnp.int32)
    source = jnp.full((slot_total * capacity,), route_total, jnp.int32)
    source = source.at[dest_index].set(jnp.arange(route_total, dtype=jnp.int32), mode="drop")
    return kept_mask, dest_index, source


def expert_apply_forward(rows_in, gate_up, down, adapt_a, adapt_b):
    adapter_rank_count = adapt_b.shape[1]
    hidden_width = adapt_b.shape[2]
    reduced_rank_rows = jnp.dot(rows_in, adapt_a, preferred_element_type=jnp.float32).astype(jnp.bfloat16)
    base_preactivation = jnp.dot(rows_in, gate_up, preferred_element_type=jnp.float32)
    adapter_gate_delta = jnp.dot(reduced_rank_rows[:, :adapter_rank_count], adapt_b[0], preferred_element_type=jnp.float32)
    adapter_up_delta = jnp.dot(reduced_rank_rows[:, adapter_rank_count:], adapt_b[1], preferred_element_type=jnp.float32)
    gate_preactivation = base_preactivation[:, :hidden_width] + ADAPTER_SCALE * adapter_gate_delta
    up_preactivation = base_preactivation[:, hidden_width:] + ADAPTER_SCALE * adapter_up_delta
    sigmoid_gate = jax.nn.sigmoid(gate_preactivation)
    active = gate_preactivation * sigmoid_gate
    hidden = (active * up_preactivation).astype(jnp.bfloat16)
    layer_output = jnp.dot(hidden, down, preferred_element_type=jnp.float32).astype(jnp.bfloat16)
    return layer_output, (reduced_rank_rows, gate_preactivation, up_preactivation, sigmoid_gate, active)


def expert_backward(rows_in, scaled, down, adapt_b, saved_residuals):
    reduced_rank_rows, gate_preactivation, up_preactivation, sigmoid_gate, active = saved_residuals
    adapter_rank_count = adapt_b.shape[1]
    back_hidden = lax.dot_general(scaled, down, (((1,), (1,)), ((), ())), preferred_element_type=jnp.float32)
    up_preactivation_gradient = (back_hidden * active).astype(jnp.bfloat16)
    slope = sigmoid_gate * (1.0 + gate_preactivation * (1.0 - sigmoid_gate))
    gate_preactivation_gradient = (back_hidden * up_preactivation * slope).astype(jnp.bfloat16)
    row_dimension_numbers = (((0,), (0,)), ((), ()))
    gate_up_map_gradient = ADAPTER_SCALE * lax.dot_general(reduced_rank_rows[:, :adapter_rank_count], gate_preactivation_gradient, row_dimension_numbers, preferred_element_type=jnp.float32)
    up_map_gradient = ADAPTER_SCALE * lax.dot_general(reduced_rank_rows[:, adapter_rank_count:], up_preactivation_gradient, row_dimension_numbers, preferred_element_type=jnp.float32)
    cols_dims = (((1,), (1,)), ((), ()))
    gate_reduced_rows = lax.dot_general(gate_preactivation_gradient, adapt_b[0], cols_dims, preferred_element_type=jnp.float32)
    up_reduced_rows = lax.dot_general(up_preactivation_gradient, adapt_b[1], cols_dims, preferred_element_type=jnp.float32)
    reduced_gradient = (ADAPTER_SCALE * jnp.concatenate([gate_reduced_rows, up_reduced_rows], axis=1)).astype(jnp.bfloat16)
    grad_adapt_a = lax.dot_general(rows_in, reduced_gradient, row_dimension_numbers, preferred_element_type=jnp.float32)
    return grad_adapt_a, jnp.stack([gate_up_map_gradient, up_map_gradient])


def reference(tokens, cotangent, routing, router_route_weights, route_replica_choice, device_expert_table, gate_up_weight, down_weight, adapter_down_maps, adapter_up_maps):
    groups = N_DP * SLOTS
    route_total = TOK_DEV * TOP
    kept_mask, dest_index, source = jax.vmap(route_rows, in_axes=(0, 0, None, None))(
        routing.reshape(groups, TOK_DEV, TOP), route_replica_choice.reshape(groups, TOK_DEV, TOP), device_expert_table, CAP)
    valid_route_mask = source < route_total
    safe_route = jnp.minimum(source, route_total - 1).astype(jnp.int32)
    block_start = (jnp.arange(groups, dtype=jnp.int32) * TOK_DEV)[:, None]
    route_token_index = (block_start + safe_route // TOP).astype(jnp.int32)
    route_weight_rows = jnp.take_along_axis(router_route_weights.reshape(groups, route_total), safe_route, axis=1)

    def grouped_by_device(table):
        return table.reshape(groups, SLOTS, CAP).transpose(1, 0, 2).reshape(SLOTS, groups * CAP)

    def per_slot(accum, element_list):
        index_row, valid_row, weight_row, gate_up, down, adapt_a, adapt_b = element_list
        zero_row = jnp.zeros((), jnp.bfloat16)
        rows_in = jnp.where(valid_row[:, None], tokens[index_row], zero_row).astype(jnp.bfloat16)
        product = (weight_row[:, None] * cotangent[index_row].astype(jnp.float32)).astype(jnp.bfloat16)
        scaled = jnp.where(valid_row[:, None], product, zero_row).astype(jnp.bfloat16)
        layer_output, saved_residuals = expert_apply_forward(rows_in, gate_up, down, adapt_a, adapt_b)
        grad_adapt_a, grad_adapt_b = expert_backward(rows_in, scaled, down, adapt_b, saved_residuals)
        contrib = jnp.where(valid_row[:, None], weight_row[:, None] * layer_output.astype(jnp.float32), jnp.zeros((), jnp.float32))
        accum = accum.at[index_row].add(contrib)
        return accum, (grad_adapt_a, grad_adapt_b)

    accum_start = jnp.zeros((TOKENS, D), jnp.float32)
    element_list = (grouped_by_device(route_token_index), grouped_by_device(valid_route_mask), grouped_by_device(route_weight_rows), gate_up_weight, down_weight, adapter_down_maps, adapter_up_maps)
    accum, (slot_a, slot_b) = lax.scan(per_slot, accum_start, element_list)
    mixed = accum.astype(jnp.bfloat16)
    same = (device_expert_table[:, None] == device_expert_table[None, :]).astype(jnp.float32)
    grad_a = jnp.dot(same, slot_a.reshape(SLOTS, -1), precision=lax.Precision.HIGHEST).reshape(slot_a.shape)
    grad_b = jnp.dot(same, slot_b.reshape(SLOTS, -1), precision=lax.Precision.HIGHEST).reshape(slot_b.shape)
    return mixed, grad_a, grad_b
```

```python
import jax
import jax.numpy as jnp
from jax import lax
from jax.sharding import PartitionSpec as P

ADAPTER_SCALE = 0.5
CAP = 16


def route_meta(routing, weights, choice, table):
    slots = table.shape[0]
    tok, top = routing.shape
    n = tok * top
    same = table[:, None] == table[None, :]
    ar = jnp.arange(slots, dtype=jnp.int32)
    occ = jnp.sum((same & (ar[None, :] < ar[:, None])).astype(jnp.int32), axis=1)
    cnt = jnp.sum(same.astype(jnp.int32), axis=1)
    holds = routing.reshape(n)[:, None] == table[None, :]
    wanted = choice.reshape(n)[:, None] % cnt[None, :]
    picked = holds & (wanted == occ[None, :])
    rows = lax.broadcasted_iota(jnp.int32, (n, n), 0)
    cols = lax.broadcasted_iota(jnp.int32, (n, n), 1)
    tri = (cols < rows).astype(jnp.bfloat16)
    ahead = jnp.dot(tri, picked.astype(jnp.bfloat16), preferred_element_type=jnp.float32)
    rank = jnp.where(picked, ahead, -1.0)
    hit = rank[:, None, :] == jnp.arange(CAP, dtype=jnp.float32)[None, :, None]
    token = (jnp.arange(n, dtype=jnp.int32) // top + 1).astype(jnp.float32)
    src = jnp.sum(jnp.where(hit, token[:, None, None], 0.0), axis=0) - 1.0
    wgt = jnp.sum(jnp.where(hit, weights.reshape(n)[:, None, None], 0.0), axis=0)
    return src.T, wgt.T


def body(tokens, cotangent, routing, weights, choice, table, gate_up, down, amap, bmap):
    slots = lax.axis_size("expert")
    n_dp = lax.axis_size("dp")
    tok, width = tokens.shape
    gate_up, down, amap, bmap = gate_up[0], down[0], amap[0], bmap[0]
    rank, ff = bmap.shape[1:]
    src, wgt = route_meta(routing, weights, choice, table)
    src, wgt = src.reshape(-1), wgt.reshape(-1)
    total = src.shape[0]
    tid = jnp.arange(tok, dtype=jnp.float32)
    onehot = (src[:, None] == tid[None, :]).astype(jnp.bfloat16)
    rows_out = jnp.dot(onehot, tokens, preferred_element_type=jnp.float32).astype(jnp.bfloat16)
    scaled_out = (
        jnp.dot(onehot, cotangent, preferred_element_type=jnp.float32) * wgt[:, None]
    ).astype(jnp.bfloat16)

    def exchange(v):
        return lax.all_to_all(v, "expert", split_axis=0, concat_axis=0, tiled=True)

    x = exchange(rows_out)
    low = jnp.dot(x, amap, preferred_element_type=jnp.float32).astype(jnp.bfloat16)
    pre = jnp.dot(x, gate_up, preferred_element_type=jnp.float32)
    pre_gate = pre[:, :ff] + ADAPTER_SCALE * jnp.dot(
        low[:, :rank], bmap[0], preferred_element_type=jnp.float32
    )
    pre_up = pre[:, ff:] + ADAPTER_SCALE * jnp.dot(
        low[:, rank:], bmap[1], preferred_element_type=jnp.float32
    )
    sig = jax.nn.sigmoid(pre_gate)
    act = pre_gate * sig
    hidden = (act * pre_up).astype(jnp.bfloat16)
    out = jnp.dot(hidden, down, preferred_element_type=jnp.float32).astype(jnp.bfloat16)
    ret = exchange(out)
    wmat = jnp.where(src[None, :] == tid[:, None], wgt[None, :], 0.0)
    w_hi = wmat.astype(jnp.bfloat16)
    w_lo = (wmat - w_hi.astype(jnp.float32)).astype(jnp.bfloat16)
    mixed = (
        jnp.dot(w_hi, ret, preferred_element_type=jnp.float32)
        + jnp.dot(w_lo, ret, preferred_element_type=jnp.float32)
    ).astype(jnp.bfloat16)

    scaled = exchange(scaled_out)
    back = lax.dot_general(scaled, down, (((1,), (1,)), ((), ())), preferred_element_type=jnp.float32)
    g_up = (back * act).astype(jnp.bfloat16)
    g_gate = (back * pre_up * (sig * (1.0 + pre_gate * (1.0 - sig)))).astype(jnp.bfloat16)
    rdims = (((0,), (0,)), ((), ()))
    cdims = (((1,), (1,)), ((), ()))
    gb0 = ADAPTER_SCALE * lax.dot_general(low[:, :rank], g_gate, rdims, preferred_element_type=jnp.float32)
    gb1 = ADAPTER_SCALE * lax.dot_general(low[:, rank:], g_up, rdims, preferred_element_type=jnp.float32)
    lg0 = lax.dot_general(g_gate, bmap[0], cdims, preferred_element_type=jnp.float32)
    lg1 = lax.dot_general(g_up, bmap[1], cdims, preferred_element_type=jnp.float32)
    low_grad = (ADAPTER_SCALE * jnp.concatenate([lg0, lg1], axis=1)).astype(jnp.bfloat16)
    ga = lax.dot_general(x, low_grad, rdims, preferred_element_type=jnp.float32)
    gb = jnp.concatenate([gb0, gb1], axis=0)
    lanes = 2 * rank
    grads = jnp.concatenate(
        [ga] + [gb[:, i * lanes : (i + 1) * lanes] for i in range(ff // lanes)], axis=0
    )
    part = lax.psum_scatter(grads, "dp", scatter_dimension=0, tiled=True)
    piece = part.reshape(slots, -1)
    got = exchange(piece)
    same = (table[:, None] == table[None, :]).astype(jnp.float32)
    summed = jnp.dot(same, got, precision=lax.Precision.HIGHEST)
    mine = exchange(summed).reshape(part.shape)
    full = lax.all_gather(mine, "dp", axis=0, tiled=True)
    grad_a = full[:width]
    grad_b = jnp.concatenate(
        [full[width + i * lanes : width + (i + 1) * lanes] for i in range(ff // lanes)], axis=1
    )
    return mixed, grad_a[None], grad_b.reshape(1, 2, rank, ff)


def solution(mesh):
    both = P(("dp", "expert"), None)
    return jax.shard_map(
        body,
        mesh=mesh,
        in_specs=(both, both, both, both, both, P(), P("expert", None, None), P("expert", None, None),
                  P("expert", None, None), P("expert", None, None, None)),
        out_specs=(both, P("expert", None, None), P("expert", None, None, None)),
        check_vma=False,
    )
```

```python
import jax
import jax.numpy as jnp
from jax import lax
from jax.experimental import pallas as pl
from jax.experimental.pallas import tpu as pltpu
from jax.sharding import PartitionSpec as P

ADAPTER_SCALE = 0.5
CAP = 16
ROW = 8
NZ = 8
BLK = 128
F32 = jnp.float32
BF16 = jnp.bfloat16
MESH = pl.DeviceIdType.MESH
RIGHT, LEFT = 0, 1


def route_meta(routing, weights, choice, table):
    slots = table.shape[0]
    tok, top = routing.shape
    n = tok * top
    same = table[:, None] == table[None, :]
    ar = jnp.arange(slots, dtype=jnp.int32)
    occ = jnp.sum((same & (ar[None, :] < ar[:, None])).astype(jnp.int32), axis=1)
    cnt = jnp.sum(same.astype(jnp.int32), axis=1)
    holds = routing.reshape(n)[:, None] == table[None, :]
    wanted = choice.reshape(n)[:, None] % cnt[None, :]
    picked = holds & (wanted == occ[None, :])
    rows = lax.broadcasted_iota(jnp.int32, (n, n), 0)
    cols = lax.broadcasted_iota(jnp.int32, (n, n), 1)
    tri = (cols < rows).astype(BF16)
    ahead = jnp.dot(tri, picked.astype(BF16), preferred_element_type=F32)
    rank = jnp.where(picked, ahead, -1.0)
    hit = rank[:, None, :] == jnp.arange(CAP, dtype=F32)[None, :, None]
    token = (jnp.arange(n, dtype=jnp.int32) // top + 1).astype(F32)
    src = jnp.sum(jnp.where(hit, token[:, None, None], 0.0), axis=0) - 1.0
    wgt = jnp.sum(jnp.where(hit, weights.reshape(n)[:, None, None], 0.0), axis=0)
    return src.T, wgt.T


def dot(a, b):
    return jnp.dot(a, b, preferred_element_type=F32)


def dot_t(a, b):
    return lax.dot_general(a, b, (((1,), (1,)), ((), ())), preferred_element_type=F32)


def t_dot(a, b):
    return lax.dot_general(a, b, (((0,), (0,)), ((), ())), preferred_element_type=F32)


def ds(i, n):
    return pl.ds(pl.multiple_of(i * n, n), n)


def kernel(
    tokens, cots, meta, pmat, gate_up, down, amap, bmap,
    mixed_out, grads_out,
    ring, metar, pick, wcol, xs, xr, outs, rets, rsr, mix,
    gu, dn, am, bm, low, act, mul, hid, grad,
    ysend, yrecv, t1, r1, r2, r2f, rb2, rb1, yq, yo,
    ld, ag_s, ag_r, mt_s, mt_r, x_s, x_r, rt_s, rt_r, rs_s, rs_r, y_s, y_r, g_s, g_r, st,
):
    width = tokens.shape[1]
    ff = dn.shape[0]
    rank2 = am.shape[1]
    n_dp = yrecv.shape[0] + 1
    part = rank2 // n_dp
    dp = lax.axis_index("dp")
    e = lax.axis_index("expert")
    z, j = e // ROW, e % ROW

    def zdev(step):
        return (dp, lax.rem(z + step + NZ, NZ) * ROW + j)

    def rowdev(i):
        return (dp, z * ROW + i)

    def dpdev(i):
        return (i, e)

    bar = pltpu.get_barrier_semaphore()
    for s in range(1, NZ):
        pl.semaphore_signal(bar, inc=1, device_id=zdev(s), device_id_type=MESH)
    for s in range(1, ROW):
        pl.semaphore_signal(bar, inc=1, device_id=rowdev(lax.rem(j + s, ROW)), device_id_type=MESH)
    for s in range(1, n_dp):
        pl.semaphore_signal(bar, inc=1, device_id=dpdev(lax.rem(dp + s, n_dp)), device_id_type=MESH)

    half = rank2 // 2
    loads = [
        pltpu.make_async_copy(tokens, ring.at[0, 0], ld.at[0]),
        pltpu.make_async_copy(cots, ring.at[1, 0], ld.at[1]),
        pltpu.make_async_copy(gate_up, gu, ld.at[2]),
        pltpu.make_async_copy(down, dn, ld.at[3]),
        pltpu.make_async_copy(amap, am, ld.at[4]),
        pltpu.make_async_copy(bmap.at[0], bm.at[0, pl.ds(0, half)], ld.at[5]),
        pltpu.make_async_copy(bmap.at[1], bm.at[1, pl.ds(half, half)], ld.at[6]),
    ]
    for c in loads:
        c.start()
    bm[0, half:, :] = jnp.zeros((half, ff), BF16)
    bm[1, :half, :] = jnp.zeros((half, ff), BF16)
    metar[0] = meta[z]
    pl.semaphore_wait(bar, NZ - 1 + ROW - 1 + n_dp - 1)

    def copy_to(src, dst, send, recv, device):
        return pltpu.make_async_remote_copy(
            src_ref=src, dst_ref=dst, send_sem=send, recv_sem=recv, device_id=device, device_id_type=MESH
        )

    def wait_bytes(ref, sem):
        pltpu.make_async_copy(ref, ref, sem).wait()

    def ring_copy(a, way, k):
        if way == RIGHT:
            frm, to, dev = (0 if k == 1 else 2 * k - 3), 2 * k - 1, zdev(1)
        else:
            frm, to, dev = 2 * k - 2, min(2 * k, NZ - 1), zdev(-1)
        src, dst = ring.at[a, frm], ring.at[a, to]
        if k == NZ // 2:
            rows = pl.ds(0 if way == RIGHT else BLK // 2, BLK // 2)
            src, dst = src.at[rows], dst.at[rows]
        return copy_to(src, dst, ag_s.at[a, way, k - 1], ag_r.at[a, way, k - 1], dev)

    def ring_start(a, k):
        ring_copy(a, RIGHT, k).start()
        ring_copy(a, LEFT, k).start()

    loads[0].wait()
    ring_start(0, 1)

    def meta_copy(s):
        place = 2 * s - 1 if s <= NZ // 2 else 2 * (NZ - s)
        dst_row = lax.rem(z + s, NZ)
        return place, copy_to(meta.at[dst_row], metar.at[place], mt_s.at[place], mt_r.at[place], zdev(s))

    metas = dict(meta_copy(s) for s in range(1, NZ))
    for c in metas.values():
        c.start()

    def prepare(p):
        srow = jnp.broadcast_to(metar[p, 0:1, :], (BLK, BLK))
        wrow = jnp.broadcast_to(metar[p, 1:2, :], (BLK, BLK))
        lane = lax.broadcasted_iota(jnp.int32, (BLK, BLK), 1).astype(F32)
        pick[p] = (srow.T == lane).astype(BF16)
        wcol[p] = wrow.T

    CT = 512

    def relay(a, p):
        def tile(i, carry):
            v = dot(pick[p], ring[a, p, :, ds(i, CT)])
            if a == 1:
                v = v * wcol[p][:, 0:1]
            xs[a, p, :, ds(i, CT)] = v.astype(BF16)
            return carry

        lax.fori_loop(0, width // CT, tile, 0)
        row_send(xs.at[a, p], xr.at[a, p], x_s.at[a, p], x_r.at[a, p])

    def row_send(src, dst, send, recv):
        mine = ds(j, CAP)
        for s in range(1, ROW):
            to = lax.rem(j + s, ROW)
            copy_to(src.at[ds(to, CAP)], dst.at[mine], send, recv, rowdev(to)).start()
        pltpu.make_async_copy(src.at[mine], dst.at[mine], recv).start()

    def row_sent(src, send):
        wait_bytes(src.at[pl.ds(0, (ROW - 1) * CAP)], send)

    FT = 256
    CH = 256

    def forward(c):
        for p in (2 * c, 2 * c + 1):
            wait_bytes(xr.at[0, p], x_r.at[0, p])
        rows = pl.ds(c * CH, CH)
        x = xr.at[0, pl.ds(2 * c, 2)]

        def xv():
            return x[...].reshape(CH, width)

        low[rows, :] = dot(xv(), am[...]).astype(BF16)

        def tile(f, carry):
            cols = ds(f, FT)
            up_cols = pl.ds(pl.multiple_of(ff + f * FT, FT), FT)
            lw = low[rows, :]
            pg = dot(xv(), gu[:, cols]) + ADAPTER_SCALE * dot(lw, bm[0, :, cols])
            pu = dot(xv(), gu[:, up_cols]) + ADAPTER_SCALE * dot(lw, bm[1, :, cols])
            sig = jax.nn.sigmoid(pg)
            ac = pg * sig
            act[rows, cols] = ac
            mul[rows, cols] = pu * (sig * (1.0 + pg * (1.0 - sig)))
            hid[:, cols] = (ac * pu).astype(BF16)
            return carry

        lax.fori_loop(0, ff // FT, tile, 0)

        def otile(i, carry):
            cols = ds(i, CT)
            o = dot(hid[...], dn[:, cols]).astype(BF16)
            outs[2 * c, :, cols] = o[:BLK]
            outs[2 * c + 1, :, cols] = o[BLK:]
            return carry

        lax.fori_loop(0, width // CT, otile, 0)

    def backward(c):
        for p in (2 * c, 2 * c + 1):
            wait_bytes(xr.at[1, p], x_r.at[1, p])
        rows = pl.ds(c * CH, CH)

        def tile(f, lg):
            cols = ds(f, FT)
            gcols = pl.ds(pl.multiple_of(width + f * FT, FT), FT)
            back = dot_t(xr[1, pl.ds(2 * c, 2)].reshape(CH, width), dn[cols, :])
            g_up = (back * act[rows, cols]).astype(BF16)
            g_gate = (back * mul[rows, cols]).astype(BF16)
            lw = low[rows, :]
            gb0 = ADAPTER_SCALE * t_dot(lw, g_gate)
            gb1 = ADAPTER_SCALE * t_dot(lw, g_up)
            gb = jnp.concatenate([gb0[:half], gb1[half:]], axis=0)
            if c == 0:
                grad[:, gcols] = gb
            else:
                grad[:, gcols] += gb
            return lg + dot_t(g_gate, bm[0, :, cols]) + dot_t(g_up, bm[1, :, cols])

        lg = lax.fori_loop(0, ff // FT, tile, jnp.zeros((CH, rank2), F32))
        lgb = (ADAPTER_SCALE * lg).astype(BF16)

        def gtile(i, carry):
            cols = ds(i, CT)
            ga = t_dot(lgb, xr[0, pl.ds(2 * c, 2), :, cols].reshape(CH, CT))
            if c == 0:
                grad[:, cols] = ga
            else:
                grad[:, cols] += ga
            return carry

        lax.fori_loop(0, width // CT, gtile, 0)

    def places(k):
        return (0,) if k == 0 else (7,) if k == NZ // 2 else (2 * k - 1, 2 * k)

    loads[1].wait()
    for a in (0, 1):
        for k in range(NZ // 2 + 1):
            if k > 0:
                ring_copy(a, RIGHT, k).wait_recv()
                ring_copy(a, LEFT, k).wait_recv()
                if k < NZ // 2:
                    ring_start(a, k + 1)
            if a == 0 and k == NZ // 2 - 1:
                ring_start(1, 1)
            for p in places(k):
                if a == 0:
                    if p > 0:
                        metas[p].wait_recv()
                    prepare(p)
                relay(a, p)
            if a == 0 and k == 1:
                for c in loads[2:]:
                    c.wait()
            if k >= 2:
                (forward if a == 0 else backward)(k - 2)
            if a == 1 and k == 0:
                forward(3)

    def ret_start(k):
        for p in places(k):
            row_send(outs.at[p], rets.at[p], rt_s.at[p], rt_r.at[p])

    ret_start(4)
    ret_start(3)
    backward(3)

    def gcast(i, carry):
        cols = ds(i, 256)
        ysend[:, cols] = grad[:, cols].astype(BF16)
        return carry

    lax.fori_loop(0, grad.shape[1] // 256, gcast, 0)

    for s in range(1, n_dp):
        to = lax.rem(dp + s, n_dp)
        copy_to(ysend.at[ds(to, part)], yrecv.at[s - 1], y_s.at[0], y_r.at[0], dpdev(to)).start()

    for p in range(NZ):
        row_sent(xs.at[0, p], x_s.at[0, p])

    def partial(p, store):
        wait_bytes(rets.at[p], rt_r.at[p])
        srow = metar[p, 0:1, :]
        tid = lax.broadcasted_iota(jnp.int32, (BLK, BLK), 0).astype(F32)
        w = jnp.where(tid == srow, metar[p, 1:2, :], 0.0)
        hi = w.astype(BF16)
        lo = (w - hi.astype(F32)).astype(BF16)

        def tile(i, carry):
            cols = ds(i, CT)
            r = rets[p, :, cols]
            store(cols, dot(hi, r) + dot(lo, r))
            return carry

        lax.fori_loop(0, width // CT, tile, 0)

    def rs_copy(way, k):
        if k == 1:
            rows = pl.ds(0 if way == RIGHT else BLK // 2, BLK // 2)
            src, dst = xs.at[0, 7, rows], rsr.at[way, 0, rows]
        else:
            p = 2 * (NZ // 2 + 1 - k) - (0 if way == RIGHT else 1)
            src, dst = xs.at[0, p], rsr.at[way, k - 1]
        return copy_to(src, dst, rs_s.at[way, k - 1], rs_r.at[way, k - 1], zdev(1 if way == RIGHT else -1))

    def rs_step(k):
        if k == 1:
            def store(cols, v):
                xs[0, 7, :, cols] = v.astype(BF16)

            partial(7, store)
            for way in (RIGHT, LEFT):
                rs_copy(way, 1).start()
            return
        for way in (RIGHT, LEFT):
            p = 2 * (NZ // 2 + 1 - k) - (0 if way == RIGHT else 1)
            rs_copy(way, k - 1).wait_recv()

            def store(cols, v, p=p, way=way):
                if k == 2:
                    h = BLK // 2
                    mine = slice(0, h) if way == RIGHT else slice(h, BLK)
                    rest = slice(h, BLK) if way == RIGHT else slice(0, h)
                    xs[0, p, mine, cols] = (v[mine] + rsr[way, 0, mine, cols].astype(F32)).astype(BF16)
                    xs[0, p, rest, cols] = v[rest].astype(BF16)
                else:
                    xs[0, p, :, cols] = (v + rsr[way, k - 2, :, cols].astype(F32)).astype(BF16)

            partial(p, store)
            rs_copy(way, k).start()

    rs_step(1)
    ret_start(2)

    wait_bytes(yrecv, y_r.at[0])
    ncol = grad.shape[1] // 128
    tiles = [(i % NZ, i // NZ, i % 2, i // 2) for i in range(2 * ncol)]
    used = tiles[-1][1] + 1
    for zz, w, h, c in tiles:
        cols = slice(c * 128, (c + 1) * 128)
        q = grad[pl.ds(pl.multiple_of(dp * part + h * 16, 16), 16), cols]
        for s in range(n_dp - 1):
            q = q + yrecv[s, h * 16 : (h + 1) * 16, cols].astype(F32)
        t1[zz, w] = q.astype(BF16)
    for i in range(2 * ncol, used * NZ):
        t1[i % NZ, i // NZ] = jnp.zeros((16, 128), BF16)
    r1[used:] = jnp.zeros((ROW - used, NZ, 16, 128), BF16)

    head = pl.ds(0, used)
    for s in range(1, NZ):
        to = lax.rem(z + s, NZ)
        copy_to(t1.at[to], r1.at[head, z], g_s.at[0], g_r.at[0], zdev(s)).start()
    pltpu.make_async_copy(t1.at[z], r1.at[head, z], g_r.at[0]).start()

    rs_step(2)
    ret_start(1)

    wait_bytes(r1.at[head], g_r.at[0])
    for s in range(1, ROW):
        to = lax.rem(j + s, ROW)
        copy_to(r1.at[to], r2.at[j], g_s.at[1], g_r.at[1], rowdev(to)).start()
    pltpu.make_async_copy(r1.at[j], r2.at[j], g_r.at[1]).start()

    rs_step(3)
    ret_start(0)

    wait_bytes(r2, g_r.at[1])
    n = ROW * NZ
    r2f[...] = r2[...].reshape(n * 16, 128).astype(F32)
    for t in range(16):
        rows = pl.ds(t, n, stride=16)
        r2f[rows, :] = dot(pmat[...], r2f[rows, :].astype(BF16))
    s2 = r2f[...].astype(BF16).reshape(ROW, NZ, 16, 128)
    r2[...] = s2
    for s in range(1, ROW):
        to = lax.rem(j + s, ROW)
        copy_to(r2.at[to], rb2.at[j], g_s.at[2], g_r.at[2], rowdev(to)).start()
    pltpu.make_async_copy(r2.at[j], rb2.at[j], g_r.at[2]).start()

    rs_step(4)

    wait_bytes(rb2, g_r.at[2])
    for s in range(1, NZ):
        to = lax.rem(z + s, NZ)
        copy_to(rb2.at[head, to], rb1.at[z], g_s.at[3], g_r.at[3], zdev(s)).start()
    pltpu.make_async_copy(rb2.at[head, z], rb1.at[z], g_r.at[3]).start()

    def keep(cols, v):
        mix[:, cols] = v

    partial(0, keep)

    wait_bytes(rb1, g_r.at[3])
    for zz, w, h, c in tiles:
        yq[h * 16 : (h + 1) * 16, c * 128 : (c + 1) * 128] = rb1[zz, w]
    for s in range(1, n_dp):
        to = lax.rem(dp + s, n_dp)
        copy_to(yq, yo.at[ds(dp, part)], y_s.at[1], y_r.at[1], dpdev(to)).start()
    pltpu.make_async_copy(yq, yo.at[ds(dp, part)], y_r.at[1]).start()

    rs_copy(RIGHT, 4).wait_recv()
    rs_copy(LEFT, 4).wait_recv()

    def final(i, carry):
        cols = ds(i, CT)
        v = mix[:, cols] + rsr[0, 3, :, cols].astype(F32) + rsr[1, 3, :, cols].astype(F32)
        outs[0, :, cols] = v.astype(BF16)
        return carry

    row_sent(outs.at[0], rt_s.at[0])
    lax.fori_loop(0, width // CT, final, 0)
    stores = [pltpu.make_async_copy(outs.at[0], mixed_out, st.at[0])]
    stores[0].start()
    wait_bytes(yo, y_r.at[1])
    stores.append(pltpu.make_async_copy(yo, grads_out, st.at[1]))
    stores[1].start()

    for a in (0, 1):
        for k in range(1, NZ // 2 + 1):
            ring_copy(a, RIGHT, k).wait_send()
            ring_copy(a, LEFT, k).wait_send()
    for c in metas.values():
        c.wait_send()
    for p in range(NZ):
        row_sent(xs.at[1, p], x_s.at[1, p])
        if p > 0:
            row_sent(outs.at[p], rt_s.at[p])
    for way in (RIGHT, LEFT):
        for k in range(1, NZ // 2 + 1):
            rs_copy(way, k).wait_send()
    wait_bytes(yrecv, y_s.at[0])
    wait_bytes(yo.at[pl.ds(0, (n_dp - 1) * part)], y_s.at[1])
    wait_bytes(rb1.at[pl.ds(0, NZ - 1)], g_s.at[0])
    wait_bytes(r2.at[pl.ds(0, ROW - 1)], g_s.at[1])
    wait_bytes(r2.at[pl.ds(0, ROW - 1)], g_s.at[2])
    wait_bytes(rb1.at[pl.ds(0, NZ - 1)], g_s.at[3])
    for c in stores:
        c.wait()


def body(tokens, cotangent, routing, weights, choice, table, gate_up, down, amap, bmap):
    n_dp = lax.axis_size("dp")
    tok, width = tokens.shape
    rank, ff = bmap.shape[2:]
    rank2 = 2 * rank
    src, wgt = route_meta(routing, weights, choice, table)
    meta = jnp.concatenate(
        [src.reshape(NZ, 1, BLK), wgt.reshape(NZ, 1, BLK), jnp.zeros((NZ, 6, BLK), F32)], axis=1
    )
    order = table.reshape(NZ, ROW).T.reshape(-1)
    pmat = (order[:, None] == order[None, :]).astype(BF16)
    gcols = width + ff
    part = rank2 // n_dp
    used = (2 * gcols // 128 + NZ - 1) // NZ
    hbm = pl.BlockSpec(memory_space=pl.ANY)
    vmem = pl.BlockSpec(memory_space=pltpu.VMEM)
    V = pltpu.VMEM
    S = pltpu.SemaphoreType.DMA
    mixed, grads = pl.pallas_call(
        kernel,
        out_shape=(
            jax.ShapeDtypeStruct((tok, width), BF16),
            jax.ShapeDtypeStruct((rank2, gcols), BF16),
        ),
        in_specs=[hbm, hbm, vmem, vmem, hbm, hbm, hbm, hbm],
        out_specs=(hbm, hbm),
        scratch_shapes=[
            V((2, NZ, BLK, width), BF16),
            V((NZ, 8, BLK), F32),
            V((NZ, BLK, BLK), BF16),
            V((NZ, BLK, BLK), F32),
            V((2, NZ, BLK, width), BF16),
            V((2, NZ, BLK, width), BF16),
            V((NZ, BLK, width), BF16),
            V((NZ, BLK, width), BF16),
            V((2, NZ // 2, BLK, width), BF16),
            V((BLK, width), F32),
            V((width, 2 * ff), BF16),
            V((ff, width), BF16),
            V((width, rank2), BF16),
            V((2, rank2, ff), BF16),
            V((NZ * BLK, rank2), BF16),
            V((NZ * BLK, ff), F32),
            V((NZ * BLK, ff), F32),
            V((256, ff), BF16),
            V((rank2, gcols), F32),
            V((rank2, gcols), BF16),
            V((n_dp - 1, part, gcols), BF16),
            V((NZ, used, 16, 128), BF16),
            V((ROW, NZ, 16, 128), BF16),
            V((ROW, NZ, 16, 128), BF16),
            V((ROW * NZ * 16, 128), F32),
            V((ROW, NZ, 16, 128), BF16),
            V((NZ, used, 16, 128), BF16),
            V((part, gcols), BF16),
            V((rank2, gcols), BF16),
            S((7,)),
            S((2, 2, NZ // 2)),
            S((2, 2, NZ // 2)),
            S((NZ,)),
            S((NZ,)),
            S((2, NZ)),
            S((2, NZ)),
            S((NZ,)),
            S((NZ,)),
            S((2, NZ // 2)),
            S((2, NZ // 2)),
            S((2,)),
            S((2,)),
            S((4,)),
            S((4,)),
            S((2,)),
        ],
        compiler_params=pltpu.CompilerParams(
            collective_id=0, has_side_effects=True, vmem_limit_bytes=62 * 2**20
        ),
        cost_estimate=pl.CostEstimate(
            flops=16 * 10**9, bytes_accessed=14 * 2**20, transcendentals=NZ * BLK * ff
        ),
        name="moe_step",
    )(tokens, cotangent, meta, pmat, gate_up[0], down[0], amap[0], bmap[0])
    grad_a = grads[:, :width].astype(F32).T
    grad_b = grads[:, width:].astype(F32).reshape(1, 2, rank, ff)
    return mixed, grad_a[None], grad_b


def solution(mesh):
    both = P(("dp", "expert"), None)
    return jax.shard_map(
        body,
        mesh=mesh,
        in_specs=(both, both, both, both, both, P(), P("expert", None, None), P("expert", None, None),
                  P("expert", None, None), P("expert", None, None, None)),
        out_specs=(both, P("expert", None, None), P("expert", None, None, None)),
        check_vma=False,
    )
```

```python
import jax
import jax.numpy as jnp
from jax import lax
from jax.experimental import pallas as pl
from jax.experimental.pallas import tpu as pltpu
from jax.sharding import PartitionSpec as P

ADAPTER_SCALE = 0.5
CAP = 16
ROW = 8
NZ = 8
BLK = 128
F32 = jnp.float32
BF16 = jnp.bfloat16
MESH = pl.DeviceIdType.MESH
RIGHT, LEFT = 0, 1


def dot(a, b):
    return jnp.dot(a, b, preferred_element_type=F32)


def dot_t(a, b):
    return lax.dot_general(a, b, (((1,), (1,)), ((), ())), preferred_element_type=F32)


def t_dot(a, b):
    return lax.dot_general(a, b, (((0,), (0,)), ((), ())), preferred_element_type=F32)


def ds(i, n):
    return pl.ds(pl.multiple_of(i * n, n), n)


def kernel(
    tokens, cots, routing, weights, choice, table, gate_up, down, amap, bmap,
    mixed_out, grad_a_out, grad_b_out,
    ring, meta, metar, pick, wcol, whl, xs, xr, outs, rets, rsr,
    gu, dn, am, bm, low, act, mul, hid, grad,
    ysend, yrecv, t1, r1, r2, r2f, rb2, rb1, yq, yo,
    ld, ag_s, ag_r, mt_s, mt_r, x_s, x_r, rt_s, rt_r, rs_s, rs_r, y_s, y_r, g_s, g_r, w_s, st,
):
    width = tokens.shape[1]
    ff = dn.shape[0]
    rank2 = am.shape[1]
    n_dp = yrecv.shape[0] + 1
    part = rank2 // n_dp
    dp = lax.axis_index("dp")
    e = lax.axis_index("expert")
    z, j = e // ROW, e % ROW

    def zdev(step):
        return (dp, lax.rem(z + step + NZ, NZ) * ROW + j)

    def rowdev(i):
        return (dp, z * ROW + i)

    def dpdev(i):
        return (i, e)

    bar = pltpu.get_barrier_semaphore()
    for s in range(1, NZ):
        pl.semaphore_signal(bar, inc=1, device_id=zdev(s), device_id_type=MESH)
    for s in range(1, ROW):
        pl.semaphore_signal(bar, inc=1, device_id=rowdev(lax.rem(j + s, ROW)), device_id_type=MESH)
    for s in range(1, n_dp):
        pl.semaphore_signal(bar, inc=1, device_id=dpdev(lax.rem(dp + s, n_dp)), device_id_type=MESH)

    rh = rank2 // 2
    loads = [
        pltpu.make_async_copy(tokens, ring.at[0, 0], ld.at[0]),
        pltpu.make_async_copy(cots, ring.at[1, 0], ld.at[1]),
        pltpu.make_async_copy(gate_up, gu, ld.at[2]),
        pltpu.make_async_copy(down, dn, ld.at[3]),
        pltpu.make_async_copy(amap, am, ld.at[4]),
        pltpu.make_async_copy(bmap.at[0], bm.at[0, pl.ds(0, rh)], ld.at[5]),
        pltpu.make_async_copy(bmap.at[1], bm.at[1, pl.ds(rh, rh)], ld.at[6]),
    ]
    for c in loads:
        c.start()
    bm[0, rh:, :] = jnp.zeros((rh, ff), BF16)
    bm[1, :rh, :] = jnp.zeros((rh, ff), BF16)

    slots = table.shape[1]
    top = routing.shape[0]
    trow = jnp.concatenate([table[...].astype(F32)] * (BLK // slots), axis=1)
    tcol = jnp.broadcast_to(trow, (BLK, BLK)).T[:slots]
    same = (tcol == trow).astype(F32)
    sub = lax.broadcasted_iota(jnp.int32, (slots, BLK), 0)
    lane = lax.broadcasted_iota(jnp.int32, (slots, BLK), 1)
    cnt = jnp.sum(jnp.where(lane < slots, same, 0.0), axis=1, keepdims=True)
    occ = jnp.sum(jnp.where(lane < sub, same, 0.0), axis=1, keepdims=True)
    picked = jnp.zeros((slots, BLK), F32)
    wsum = jnp.zeros((slots, BLK), F32)
    for k in range(top):
        want = choice[k : k + 1, :].astype(F32)
        want = want - cnt * jnp.floor((want + 0.5) / cnt)
        hit = (tcol == routing[k : k + 1, :].astype(F32)) & (want == occ)
        picked = jnp.where(hit, 1.0, picked)
        wsum = jnp.where(hit, weights[k : k + 1, :], wsum)
    tri = lax.broadcasted_iota(jnp.int32, (BLK, BLK), 0) < lax.broadcasted_iota(jnp.int32, (BLK, BLK), 1)
    ahead = dot(picked.astype(BF16), tri.astype(F32).astype(BF16))
    rank = jnp.where(picked > 0.0, ahead, -1.0)
    for i in range(NZ):
        meta[i, :ROW] = rank[i * ROW : (i + 1) * ROW]
        meta[i, ROW:] = wsum[i * ROW : (i + 1) * ROW]
    metar[0] = meta[z]
    pl.semaphore_wait(bar, NZ - 1 + ROW - 1 + n_dp - 1)

    def copy_to(src, dst, send, recv, device):
        return pltpu.make_async_remote_copy(
            src_ref=src, dst_ref=dst, send_sem=send, recv_sem=recv, device_id=device, device_id_type=MESH
        )

    def wait_bytes(ref, sem):
        pltpu.make_async_copy(ref, ref, sem).wait()

    HW = width // 2

    def half(h):
        return pl.ds(h * HW, HW)

    def ring_copy(a, way, k, h):
        if way == RIGHT:
            frm, to, dev = (0 if k == 1 else 2 * k - 3), 2 * k - 1, zdev(1)
        else:
            frm, to, dev = 2 * k - 2, min(2 * k, NZ - 1), zdev(-1)
        rows = pl.ds(0, BLK)
        if k == NZ // 2:
            rows = pl.ds(0 if way == RIGHT else BLK // 2, BLK // 2)
        src, dst = ring.at[a, frm, rows, half(h)], ring.at[a, to, rows, half(h)]
        return copy_to(src, dst, ag_s.at[a, way, k - 1, h], ag_r.at[a, way, k - 1, h], dev)

    def ring_start(a, k, h):
        ring_copy(a, RIGHT, k, h).start()
        ring_copy(a, LEFT, k, h).start()

    loads[0].wait()
    ring_start(0, 1, 0)
    ring_start(0, 1, 1)

    def meta_copy(s):
        place = 2 * s - 1 if s <= NZ // 2 else 2 * (NZ - s)
        dst_row = lax.rem(z + s, NZ)
        return place, copy_to(meta.at[dst_row], metar.at[place], mt_s.at[place], mt_r.at[place], zdev(s))

    metas = dict(meta_copy(s) for s in range(1, NZ))
    for c in metas.values():
        c.start()

    def prepare(p):
        order = lax.broadcasted_iota(jnp.int32, (CAP, BLK), 0).astype(F32)
        parts = []
        for i in range(ROW):
            rows = slice(i * CAP, (i + 1) * CAP)
            hit = jnp.broadcast_to(metar[p, i : i + 1, :], (CAP, BLK)) == order
            pick[p, rows] = jnp.where(hit, 1.0, 0.0).astype(BF16)
            w = jnp.where(hit, jnp.broadcast_to(metar[p, ROW + i : ROW + i + 1, :], (CAP, BLK)), 0.0)
            wcol[p, rows] = jnp.broadcast_to(jnp.sum(w, axis=1, keepdims=True), (CAP, BLK))
            parts.append(w)
        wt = jnp.concatenate(parts, axis=0).T
        hi = wt.astype(BF16)
        whl[p, 0] = hi
        whl[p, 1] = (wt - hi.astype(F32)).astype(BF16)

    CT = 512

    def relay(a, p, h):
        def tile(i, carry):
            cols = pl.ds(pl.multiple_of(h * HW + i * CT, CT), CT)
            v = dot(pick[p], ring[a, p, :, cols])
            if a == 1:
                v = v * wcol[p][:, 0:1]
            xs[a, p, :, cols] = v.astype(BF16)
            return carry

        lax.fori_loop(0, HW // CT, tile, 0)
        row_send(xs.at[a, p, :, half(h)], xr.at[a, p, :, half(h)], x_s.at[a, p, h], x_r.at[a, p, h])

    def rows_here(a, p):
        for h in (0, 1):
            wait_bytes(xr.at[a, p, :, half(h)], x_r.at[a, p, h])

    def rows_gone(a, p):
        for h in (0, 1):
            row_sent(xs.at[a, p, :, half(h)], x_s.at[a, p, h])

    def row_send(src, dst, send, recv):
        mine = ds(j, CAP)
        for s in range(1, ROW):
            to = lax.rem(j + s, ROW)
            copy_to(src.at[ds(to, CAP)], dst.at[mine], send, recv, rowdev(to)).start()
        pltpu.make_async_copy(src.at[mine], dst.at[mine], recv).start()

    def row_sent(src, send):
        wait_bytes(src.at[pl.ds(0, (ROW - 1) * CAP)], send)

    FT = 256
    CH = 256

    def forward(c):
        for p in (2 * c, 2 * c + 1):
            rows_here(0, p)
        rows = pl.ds(c * CH, CH)
        x = xr.at[0, pl.ds(2 * c, 2)]

        def xv():
            return x[...].reshape(CH, width)

        low[rows, :] = dot(xv(), am[...]).astype(BF16)

        def tile(f, carry):
            cols = ds(f, FT)
            up_cols = pl.ds(pl.multiple_of(ff + f * FT, FT), FT)
            lw = low[rows, :]
            pg = dot(xv(), gu[:, cols]) + ADAPTER_SCALE * dot(lw, bm[0, :, cols])
            pu = dot(xv(), gu[:, up_cols]) + ADAPTER_SCALE * dot(lw, bm[1, :, cols])
            sig = jax.nn.sigmoid(pg)
            ac = pg * sig
            act[rows, cols] = ac
            mul[rows, cols] = pu * (sig * (1.0 + pg * (1.0 - sig)))
            hid[:, cols] = (ac * pu).astype(BF16)
            return carry

        lax.fori_loop(0, ff // FT, tile, 0)

        def otile(i, carry):
            cols = ds(i, CT)
            o = dot(hid[...], dn[:, cols]).astype(BF16)
            outs[2 * c, :, cols] = o[:BLK]
            outs[2 * c + 1, :, cols] = o[BLK:]
            return carry

        lax.fori_loop(0, width // CT, otile, 0)

    def backward(c):
        for p in (2 * c, 2 * c + 1):
            rows_here(1, p)
        rows = pl.ds(c * CH, CH)

        def tile(f, lg):
            cols = ds(f, FT)
            gcols = pl.ds(pl.multiple_of(width + f * FT, FT), FT)
            back = dot_t(xr[1, pl.ds(2 * c, 2)].reshape(CH, width), dn[cols, :])
            g_up = (back * act[rows, cols]).astype(BF16)
            g_gate = (back * mul[rows, cols]).astype(BF16)
            lw = low[rows, :]
            gb0 = ADAPTER_SCALE * t_dot(lw, g_gate)
            gb1 = ADAPTER_SCALE * t_dot(lw, g_up)
            gb = jnp.concatenate([gb0[:rh], gb1[rh:]], axis=0)
            if c == 0:
                grad[:, gcols] = gb
            else:
                grad[:, gcols] += gb
            return lg + dot_t(g_gate, bm[0, :, cols]) + dot_t(g_up, bm[1, :, cols])

        lg = lax.fori_loop(0, ff // FT, tile, jnp.zeros((CH, rank2), F32))
        lgb = (ADAPTER_SCALE * lg).astype(BF16)

        def gtile(i, carry):
            cols = ds(i, CT)
            ga = t_dot(lgb, xr[0, pl.ds(2 * c, 2), :, cols].reshape(CH, CT))
            if c == 0:
                grad[:, cols] = ga
            else:
                grad[:, cols] += ga
            return carry

        lax.fori_loop(0, width // CT, gtile, 0)

    def places(k):
        return (0,) if k == 0 else (7,) if k == NZ // 2 else (2 * k - 1, 2 * k)

    prepare(0)
    for h in (0, 1):
        relay(0, 0, h)
    loads[1].wait()
    for h in (0, 1):
        relay(1, 0, h)
    for a in (0, 1):
        for k in range(1, NZ // 2 + 1):
            for h in (0, 1):
                ring_copy(a, RIGHT, k, h).wait_recv()
                ring_copy(a, LEFT, k, h).wait_recv()
                if k < NZ // 2:
                    ring_start(a, k + 1, h)
                if a == 0 and k == NZ // 2 - 1 and h == 1:
                    ring_start(1, 1, 0)
                    ring_start(1, 1, 1)
                for p in places(k):
                    if a == 0 and h == 0:
                        metas[p].wait_recv()
                        prepare(p)
                    relay(a, p, h)
            if a == 0 and k == 1:
                for c in loads[2:]:
                    c.wait()
            if a == 0 and k >= 2:
                forward(k - 2)
            if a == 1 and k == 1:
                forward(3)
            if a == 1 and k in (2, 3):
                backward(k - 2)

    groups = [(h, k) for k in range(NZ // 2, -1, -1) for h in (0, 1)]

    def ret_refs(h, p):
        return outs.at[p, :, half(h)], rets.at[p, :, half(h)], rt_s.at[h, p], rt_r.at[h, p]

    def ret_start(g):
        if g >= len(groups):
            return
        h, k = groups[g]
        for p in places(k):
            row_send(*ret_refs(h, p))

    GP = grad.shape[1] // 2
    NT = 2 * GP // 128
    WT = (NT + NZ - 1) // NZ

    def piece(q):
        return pl.ds(q * GP, GP)

    def dp_send(q):
        ysend[:, piece(q)] = grad[:, piece(q)].astype(BF16)
        for s in range(1, n_dp):
            to = lax.rem(dp + s, n_dp)
            copy_to(
                ysend.at[ds(to, part), piece(q)], yrecv.at[s - 1, :, piece(q)], y_s.at[0, q], y_r.at[0, q], dpdev(to)
            ).start()

    def tiles(q):
        return [(i % NZ, q * WT + i // NZ, i % 2, q * (NT // 2) + i // 2) for i in range(NT)]

    def owners(q):
        return pl.ds(q * WT, WT)

    def z_send(q):
        wait_bytes(yrecv.at[:, :, piece(q)], y_r.at[0, q])
        for zz, w, hh, c in tiles(q):
            cols = slice(c * 128, (c + 1) * 128)
            v = grad[pl.ds(pl.multiple_of(dp * part + hh * 16, 16), 16), cols]
            for s in range(n_dp - 1):
                v = v + yrecv[s, hh * 16 : (hh + 1) * 16, cols].astype(F32)
            t1[zz, w] = v.astype(BF16)
        for i in range(NT, WT * NZ):
            t1[i % NZ, q * WT + i // NZ] = jnp.zeros((16, 128), BF16)
        for s in range(1, NZ):
            to = lax.rem(z + s, NZ)
            copy_to(t1.at[to, owners(q)], r1.at[owners(q), z], g_s.at[0, q], g_r.at[0, q], zdev(s)).start()
        pltpu.make_async_copy(t1.at[z, owners(q)], r1.at[owners(q), z], g_r.at[0, q]).start()

    def row_copy(w):
        return copy_to(r1.at[w], r2.at[:, j], w_s.at[w], g_r.at[1, 0], rowdev(w))

    def x_send(q):
        wait_bytes(r1.at[owners(q)], g_r.at[0, q])
        for w in range(q * WT, (q + 1) * WT):

            @pl.when(j != w)
            def _(w=w):
                row_copy(w).start()

            @pl.when(j == w)
            def _(w=w):
                pltpu.make_async_copy(r1.at[w], r2.at[:, j], g_r.at[1, 0]).start()

    def owner(q):
        return (j >= q * WT) & (j < (q + 1) * WT)

    def x_sum(q):
        @pl.when(owner(q))
        def _():
            wait_bytes(r2, g_r.at[1, 0])
            pm = same[:, :slots].astype(BF16)
            r2f[...] = r2[...].reshape(slots * 16, 128).astype(F32)
            for t in range(16):
                rows = pl.ds(t, slots, stride=16)
                r2f[rows, :] = dot(pm, r2f[rows, :].astype(BF16))
            r2[...] = r2f[...].astype(BF16).reshape(NZ, ROW, 16, 128)
            for s in range(1, ROW):
                to = lax.rem(j + s, ROW)
                copy_to(r2.at[:, to], rb2.at[j], g_s.at[1, 0], g_r.at[2, q], rowdev(to)).start()
            pltpu.make_async_copy(r2.at[:, j], rb2.at[j], g_r.at[2, q]).start()

    def z_back(q):
        wait_bytes(rb2.at[owners(q)], g_r.at[2, q])
        for s in range(1, NZ):
            to = lax.rem(z + s, NZ)
            copy_to(rb2.at[owners(q), to], rb1.at[z, owners(q)], g_s.at[2, q], g_r.at[3, q], zdev(s)).start()
        pltpu.make_async_copy(rb2.at[owners(q), z], rb1.at[z, owners(q)], g_r.at[3, q]).start()

    def dp_back(q):
        wait_bytes(rb1.at[:, owners(q)], g_r.at[3, q])
        for zz, w, hh, c in tiles(q):
            yq[hh * 16 : (hh + 1) * 16, c * 128 : (c + 1) * 128] = rb1[zz, w]
        dst = yo.at[ds(dp, part), piece(q)]
        for s in range(1, n_dp):
            to = lax.rem(dp + s, n_dp)
            copy_to(yq.at[:, piece(q)], dst, y_s.at[1, q], y_r.at[1, q], dpdev(to)).start()
        pltpu.make_async_copy(yq.at[:, piece(q)], dst, y_r.at[1, q]).start()

    def turn(first, last):
        def block(i, carry):
            am[ds(i, BLK), :] = yo[:, ds(i, BLK)].astype(F32).T.astype(BF16)
            return carry

        lax.fori_loop(first, last, block, 0)

    def partial(h, p, store):
        _, dst, _, recv = ret_refs(h, p)
        wait_bytes(dst, recv)

        def tile(i, carry):
            cols = pl.ds(pl.multiple_of(h * HW + i * CT, CT), CT)
            r = rets[p, :, cols]
            store(cols, dot(whl[p, 0], r) + dot(whl[p, 1], r))
            return carry

        lax.fori_loop(0, HW // CT, tile, 0)

    def rs_copy(h, way, k):
        if k == 1:
            rows = pl.ds(0 if way == RIGHT else BLK // 2, BLK // 2)
            src, dst = xs.at[0, 7, rows, half(h)], rsr.at[way, 0, rows, half(h)]
        else:
            p = 2 * (NZ // 2 + 1 - k) - (0 if way == RIGHT else 1)
            src, dst = xs.at[0, p, :, half(h)], rsr.at[way, k - 1, :, half(h)]
        return copy_to(src, dst, rs_s.at[h, way, k - 1], rs_r.at[h, way, k - 1], zdev(1 if way == RIGHT else -1))

    def rs_step(h, k):
        if k == 1:

            def store(cols, v):
                xs[0, 7, :, cols] = v.astype(BF16)

            partial(h, 7, store)
            for way in (RIGHT, LEFT):
                rs_copy(h, way, 1).start()
            return
        for way in (RIGHT, LEFT):
            p = 2 * (NZ // 2 + 1 - k) - (0 if way == RIGHT else 1)
            rs_copy(h, way, k - 1).wait_recv()

            def store(cols, v, p=p, way=way):
                if k == 2:
                    m = BLK // 2
                    mine = slice(0, m) if way == RIGHT else slice(m, BLK)
                    rest = slice(m, BLK) if way == RIGHT else slice(0, m)
                    xs[0, p, mine, cols] = (v[mine] + rsr[way, 0, mine, cols].astype(F32)).astype(BF16)
                    xs[0, p, rest, cols] = v[rest].astype(BF16)
                else:
                    xs[0, p, :, cols] = (v + rsr[way, k - 2, :, cols].astype(F32)).astype(BF16)

            partial(h, p, store)
            rs_copy(h, way, k).start()

    def rs_last(h):
        for way in (RIGHT, LEFT):
            rs_copy(h, way, NZ // 2).wait_recv()
        src, _, send, _ = ret_refs(h, 0)
        row_sent(src, send)

        def store(cols, v):
            v = v + rsr[0, 3, :, cols].astype(F32) + rsr[1, 3, :, cols].astype(F32)
            outs[0, :, cols] = v.astype(BF16)

        partial(h, 0, store)
        c = pltpu.make_async_copy(outs.at[0, :, half(h)], mixed_out.at[:, half(h)], st.at[h])
        c.start()
        stores.append(c)

    stores = []

    def store_out(src, dst, i):
        c = pltpu.make_async_copy(src, dst, st.at[i])
        c.start()
        stores.append(c)

    for g in range(3):
        ret_start(g)
    backward(2)
    rows_gone(0, 7)
    rs_step(0, 1)
    backward(3)
    dp_send(0)
    dp_send(1)
    rs_step(1, 1)
    ret_start(3)
    for p in range(NZ - 1):
        rows_gone(0, p)
    rs_step(0, 2)
    ret_start(4)
    z_send(0)
    rs_step(1, 2)
    ret_start(5)
    z_send(1)
    x_send(0)
    rs_step(0, 3)
    ret_start(6)
    x_send(1)
    rs_step(1, 3)
    ret_start(7)
    x_sum(0)
    rs_step(0, 4)
    ret_start(8)
    ret_start(9)
    x_sum(1)
    z_back(0)
    rs_step(1, 4)
    z_back(1)
    dp_back(0)
    rs_last(0)
    rs_last(1)
    dp_back(1)
    cut = GP // BLK
    wait_bytes(yo.at[:, piece(0)], y_r.at[1, 0])
    turn(0, cut)
    wait_bytes(yo.at[:, piece(1)], y_r.at[1, 1])
    store_out(yo.at[:, pl.ds(width, ff)], grad_b_out, 3)
    turn(cut, width // BLK)
    store_out(am, grad_a_out, 2)

    for a in (0, 1):
        for k in range(1, NZ // 2 + 1):
            for h in (0, 1):
                ring_copy(a, RIGHT, k, h).wait_send()
                ring_copy(a, LEFT, k, h).wait_send()
    for c in metas.values():
        c.wait_send()
    for p in range(NZ):
        rows_gone(1, p)
        for h in (0, 1):
            if p > 0:
                src, _, send, _ = ret_refs(h, p)
                row_sent(src, send)
    for h in (0, 1):
        for way in (RIGHT, LEFT):
            for k in range(1, NZ // 2 + 1):
                rs_copy(h, way, k).wait_send()
    for q in (0, 1):
        wait_bytes(yrecv.at[:, :, piece(q)], y_s.at[0, q])
        wait_bytes(yo.at[pl.ds(0, (n_dp - 1) * part), piece(q)], y_s.at[1, q])
        wait_bytes(rb1.at[pl.ds(0, NZ - 1), owners(q)], g_s.at[0, q])
        wait_bytes(rb1.at[pl.ds(0, NZ - 1), owners(q)], g_s.at[2, q])
        for w in range(q * WT, (q + 1) * WT):

            @pl.when(j != w)
            def _(w=w):
                row_copy(w).wait_send()

        @pl.when(owner(q))
        def _():
            wait_bytes(r1.at[pl.ds(0, ROW - 1)], g_s.at[1, 0])

    for c in stores:
        c.wait()


def body(tokens, cotangent, routing, weights, choice, table, gate_up, down, amap, bmap):
    n_dp = lax.axis_size("dp")
    tok, width = tokens.shape
    rank, ff = bmap.shape[2:]
    rank2 = 2 * rank
    gcols = width + ff
    part = rank2 // n_dp
    used = (2 * gcols // 128 + NZ - 1) // NZ
    hbm = pl.BlockSpec(memory_space=pl.ANY)
    vmem = pl.BlockSpec(memory_space=pltpu.VMEM)
    V = pltpu.VMEM
    S = pltpu.SemaphoreType.DMA
    mixed, grad_a, grad_b = pl.pallas_call(
        kernel,
        out_shape=(
            jax.ShapeDtypeStruct((tok, width), BF16),
            jax.ShapeDtypeStruct((width, rank2), BF16),
            jax.ShapeDtypeStruct((rank2, ff), BF16),
        ),
        in_specs=[hbm, hbm, vmem, vmem, vmem, vmem, hbm, hbm, hbm, hbm],
        out_specs=(hbm, hbm, hbm),
        scratch_shapes=[
            V((2, NZ, BLK, width), BF16),
            V((NZ, 2 * ROW, BLK), F32),
            V((NZ, 2 * ROW, BLK), F32),
            V((NZ, BLK, BLK), BF16),
            V((NZ, BLK, BLK), F32),
            V((NZ, 2, BLK, BLK), BF16),
            V((2, NZ, BLK, width), BF16),
            V((2, NZ, BLK, width), BF16),
            V((NZ, BLK, width), BF16),
            V((NZ, BLK, width), BF16),
            V((2, NZ // 2, BLK, width), BF16),
            V((width, 2 * ff), BF16),
            V((ff, width), BF16),
            V((width, rank2), BF16),
            V((2, rank2, ff), BF16),
            V((NZ * BLK, rank2), BF16),
            V((NZ * BLK, ff), F32),
            V((NZ * BLK, ff), F32),
            V((256, ff), BF16),
            V((rank2, gcols), F32),
            V((rank2, gcols), BF16),
            V((n_dp - 1, part, gcols), BF16),
            V((NZ, used, 16, 128), BF16),
            V((ROW, NZ, 16, 128), BF16),
            V((ROW, NZ, 16, 128), BF16),
            V((ROW * NZ * 16, 128), F32),
            V((ROW, NZ, 16, 128), BF16),
            V((NZ, used, 16, 128), BF16),
            V((part, gcols), BF16),
            V((rank2, gcols), BF16),
            S((7,)),
            S((2, 2, NZ // 2, 2)),
            S((2, 2, NZ // 2, 2)),
            S((NZ,)),
            S((NZ,)),
            S((2, NZ, 2)),
            S((2, NZ, 2)),
            S((2, NZ)),
            S((2, NZ)),
            S((2, 2, NZ // 2)),
            S((2, 2, NZ // 2)),
            S((2, 2)),
            S((2, 2)),
            S((3, 2)),
            S((4, 2)),
            S((used,)),
            S((4,)),
        ],
        compiler_params=pltpu.CompilerParams(
            collective_id=0, has_side_effects=True, vmem_limit_bytes=62 * 2**20
        ),
        cost_estimate=pl.CostEstimate(
            flops=16 * 10**9, bytes_accessed=14 * 2**20, transcendentals=NZ * BLK * ff
        ),
        name="moe_step",
    )(
        tokens, cotangent, routing.T, weights.T, choice.T, table.reshape(1, -1),
        gate_up[0], down[0], amap[0], bmap[0],
    )
    return mixed, grad_a.astype(F32)[None], grad_b.astype(F32).reshape(1, 2, rank, ff)


def solution(mesh):
    both = P(("dp", "expert"), None)
    return jax.shard_map(
        body,
        mesh=mesh,
        in_specs=(both, both, both, both, both, P(), P("expert", None, None), P("expert", None, None),
                  P("expert", None, None), P("expert", None, None, None)),
        out_specs=(both, P("expert", None, None), P("expert", None, None, None)),
        check_vma=False,
    )
```

```python
import jax
import jax.numpy as jnp
from jax import lax
from jax.experimental import pallas as pl
from jax.experimental.pallas import tpu as pltpu
from jax.sharding import PartitionSpec as P

ADAPTER_SCALE = 0.5
CAP = 16
ROW = 8
NZ = 8
BLK = 128
F32 = jnp.float32
BF16 = jnp.bfloat16
MESH = pl.DeviceIdType.MESH
RIGHT, LEFT = 0, 1


def dot(a, b):
    return jnp.dot(a, b, preferred_element_type=F32)


def dot_t(a, b):
    return lax.dot_general(a, b, (((1,), (1,)), ((), ())), preferred_element_type=F32)


def t_dot(a, b):
    return lax.dot_general(a, b, (((0,), (0,)), ((), ())), preferred_element_type=F32)


def ds(i, n):
    return pl.ds(pl.multiple_of(i * n, n), n)


def kernel(
    tokens, cots, routing, weights, choice, table, gate_up, down, amap, bmap,
    mixed_out, grad_a_out, grad_b_out,
    ring, meta, metar, pick, wcol, whl, xs, xr, outs, rets, rsr,
    gu, dn, am, bm, low, act, mul, hid, grad,
    ysend, yrecv, t1, r1, r2, r2f, rb2, rb1, yq, yo,
    ld, ag_s, ag_r, mt_s, mt_r, x_s, x_r, rt_s, rt_r, rs_s, rs_r, y_s, y_r, g_s, g_r, w_s, st,
):
    width = tokens.shape[1]
    ff = dn.shape[0]
    rank2 = am.shape[1]
    n_dp = yrecv.shape[0] + 1
    part = rank2 // n_dp
    dp = lax.axis_index("dp")
    e = lax.axis_index("expert")
    z, j = e // ROW, e % ROW

    def zdev(step):
        return (dp, lax.rem(z + step + NZ, NZ) * ROW + j)

    def rowdev(i):
        return (dp, z * ROW + i)

    def dpdev(i):
        return (i, e)

    bar = pltpu.get_barrier_semaphore()
    for s in range(1, NZ):
        pl.semaphore_signal(bar, inc=1, device_id=zdev(s), device_id_type=MESH)
    for s in range(1, ROW):
        pl.semaphore_signal(bar, inc=1, device_id=rowdev(lax.rem(j + s, ROW)), device_id_type=MESH)
    for s in range(1, n_dp):
        pl.semaphore_signal(bar, inc=1, device_id=dpdev(lax.rem(dp + s, n_dp)), device_id_type=MESH)

    rh = rank2 // 2
    loads = [
        pltpu.make_async_copy(tokens, ring.at[0, 0], ld.at[0]),
        pltpu.make_async_copy(cots, ring.at[1, 0], ld.at[1]),
        pltpu.make_async_copy(gate_up, gu, ld.at[2]),
        pltpu.make_async_copy(down, dn, ld.at[3]),
        pltpu.make_async_copy(amap, am, ld.at[4]),
        pltpu.make_async_copy(bmap.at[0], bm.at[0, pl.ds(0, rh)], ld.at[5]),
        pltpu.make_async_copy(bmap.at[1], bm.at[1, pl.ds(rh, rh)], ld.at[6]),
    ]
    for c in loads:
        c.start()
    bm[0, rh:, :] = jnp.zeros((rh, ff), BF16)
    bm[1, :rh, :] = jnp.zeros((rh, ff), BF16)

    slots = table.shape[1]
    top = routing.shape[0]
    trow = jnp.concatenate([table[...].astype(F32)] * (BLK // slots), axis=1)
    tcol = jnp.broadcast_to(trow, (BLK, BLK)).T[:slots]
    same = (tcol == trow).astype(F32)
    sub = lax.broadcasted_iota(jnp.int32, (slots, BLK), 0)
    lane = lax.broadcasted_iota(jnp.int32, (slots, BLK), 1)
    cnt = jnp.sum(jnp.where(lane < slots, same, 0.0), axis=1, keepdims=True)
    occ = jnp.sum(jnp.where(lane < sub, same, 0.0), axis=1, keepdims=True)
    picked = jnp.zeros((slots, BLK), F32)
    wsum = jnp.zeros((slots, BLK), F32)
    for k in range(top):
        want = choice[k : k + 1, :].astype(F32)
        want = want - cnt * jnp.floor((want + 0.5) / cnt)
        hit = (tcol == routing[k : k + 1, :].astype(F32)) & (want == occ)
        picked = jnp.where(hit, 1.0, picked)
        wsum = jnp.where(hit, weights[k : k + 1, :], wsum)
    tri = lax.broadcasted_iota(jnp.int32, (BLK, BLK), 0) < lax.broadcasted_iota(jnp.int32, (BLK, BLK), 1)
    ahead = dot(picked.astype(BF16), tri.astype(F32).astype(BF16))
    rank = jnp.where(picked > 0.0, ahead, -1.0)
    for i in range(NZ):
        meta[i, :ROW] = rank[i * ROW : (i + 1) * ROW]
        meta[i, ROW:] = wsum[i * ROW : (i + 1) * ROW]
    metar[0] = meta[z]
    pl.semaphore_wait(bar, NZ - 1 + ROW - 1 + n_dp - 1)

    def copy_to(src, dst, send, recv, device):
        return pltpu.make_async_remote_copy(
            src_ref=src, dst_ref=dst, send_sem=send, recv_sem=recv, device_id=device, device_id_type=MESH
        )

    def wait_bytes(ref, sem):
        pltpu.make_async_copy(ref, ref, sem).wait()

    HW = width // 2

    def half(h):
        return pl.ds(h * HW, HW)

    def ring_copy(a, way, k, h):
        if way == RIGHT:
            frm, to, dev = (0 if k == 1 else 2 * k - 3), 2 * k - 1, zdev(1)
        else:
            frm, to, dev = 2 * k - 2, min(2 * k, NZ - 1), zdev(-1)
        rows = pl.ds(0, BLK)
        if k == NZ // 2:
            rows = pl.ds(0 if way == RIGHT else BLK // 2, BLK // 2)
        src, dst = ring.at[a, frm, rows, half(h)], ring.at[a, to, rows, half(h)]
        return copy_to(src, dst, ag_s.at[a, way, k - 1, h], ag_r.at[a, way, k - 1, h], dev)

    def ring_start(a, k, h):
        ring_copy(a, RIGHT, k, h).start()
        ring_copy(a, LEFT, k, h).start()

    loads[0].wait()
    ring_start(0, 1, 0)
    ring_start(0, 1, 1)

    def meta_copy(s):
        place = 2 * s - 1 if s <= NZ // 2 else 2 * (NZ - s)
        dst_row = lax.rem(z + s, NZ)
        return place, copy_to(meta.at[dst_row], metar.at[place], mt_s.at[place], mt_r.at[place], zdev(s))

    metas = dict(meta_copy(s) for s in range(1, NZ))
    for c in metas.values():
        c.start()

    def prepare(p):
        order = lax.broadcasted_iota(jnp.int32, (CAP, BLK), 0).astype(F32)
        parts = []
        for i in range(ROW):
            rows = slice(i * CAP, (i + 1) * CAP)
            hit = jnp.broadcast_to(metar[p, i : i + 1, :], (CAP, BLK)) == order
            pick[p, rows] = jnp.where(hit, 1.0, 0.0).astype(BF16)
            w = jnp.where(hit, jnp.broadcast_to(metar[p, ROW + i : ROW + i + 1, :], (CAP, BLK)), 0.0)
            wcol[p, rows] = jnp.broadcast_to(jnp.sum(w, axis=1, keepdims=True), (CAP, BLK))
            parts.append(w)
        wt = jnp.concatenate(parts, axis=0).T
        hi = wt.astype(BF16)
        whl[p, 0] = hi
        whl[p, 1] = (wt - hi.astype(F32)).astype(BF16)

    CT = 512

    def relay(a, p, h):
        def tile(i, carry):
            cols = pl.ds(pl.multiple_of(h * HW + i * CT, CT), CT)
            v = dot(pick[p], ring[a, p, :, cols])
            if a == 1:
                v = v * wcol[p][:, 0:1]
            xs[a, p, :, cols] = v.astype(BF16)
            return carry

        lax.fori_loop(0, HW // CT, tile, 0)
        row_send(xs.at[a, p, :, half(h)], xr.at[a, p, :, half(h)], x_s.at[a, p, h], x_r.at[a, p, h])

    def rows_here(a, p):
        for h in (0, 1):
            wait_bytes(xr.at[a, p, :, half(h)], x_r.at[a, p, h])

    def rows_gone(a, p):
        for h in (0, 1):
            row_sent(xs.at[a, p, :, half(h)], x_s.at[a, p, h])

    def row_send(src, dst, send, recv):
        mine = ds(j, CAP)
        for s in range(1, ROW):
            to = lax.rem(j + s, ROW)
            copy_to(src.at[ds(to, CAP)], dst.at[mine], send, recv, rowdev(to)).start()
        pltpu.make_async_copy(src.at[mine], dst.at[mine], recv).start()

    def row_sent(src, send):
        wait_bytes(src.at[pl.ds(0, (ROW - 1) * CAP)], send)

    FT = 256
    CH = 256

    def forward(c):
        for p in (2 * c, 2 * c + 1):
            rows_here(0, p)
        rows = pl.ds(c * CH, CH)
        x = xr.at[0, pl.ds(2 * c, 2)]

        def xv():
            return x[...].reshape(CH, width)

        low[rows, :] = dot(xv(), am[...]).astype(BF16)

        def tile(f, carry):
            cols = ds(f, FT)
            up_cols = pl.ds(pl.multiple_of(ff + f * FT, FT), FT)
            lw = low[rows, :]
            pg = dot(xv(), gu[:, cols]) + ADAPTER_SCALE * dot(lw, bm[0, :, cols])
            pu = dot(xv(), gu[:, up_cols]) + ADAPTER_SCALE * dot(lw, bm[1, :, cols])
            sig = jax.nn.sigmoid(pg)
            ac = pg * sig
            act[rows, cols] = ac
            mul[rows, cols] = pu * (sig * (1.0 + pg * (1.0 - sig)))
            hid[:, cols] = (ac * pu).astype(BF16)
            return carry

        lax.fori_loop(0, ff // FT, tile, 0)

        def otile(i, carry):
            cols = ds(i, CT)
            o = dot(hid[...], dn[:, cols]).astype(BF16)
            outs[2 * c, :, cols] = o[:BLK]
            outs[2 * c + 1, :, cols] = o[BLK:]
            return carry

        lax.fori_loop(0, width // CT, otile, 0)

    def backward(first, n):
        for p in range(first, first + n):
            rows_here(1, p)
        nr = n * BLK
        rows = pl.ds(first * BLK, nr)

        def tile(f, lg):
            cols = ds(f, FT)
            gcols = pl.ds(pl.multiple_of(width + f * FT, FT), FT)
            back = dot_t(xr[1, pl.ds(first, n)].reshape(nr, width), dn[cols, :])
            g_up = (back * act[rows, cols]).astype(BF16)
            g_gate = (back * mul[rows, cols]).astype(BF16)
            lw = low[rows, :]
            gb0 = ADAPTER_SCALE * t_dot(lw, g_gate)
            gb1 = ADAPTER_SCALE * t_dot(lw, g_up)
            gb = jnp.concatenate([gb0[:rh], gb1[rh:]], axis=0)
            if first == 0:
                grad[:, gcols] = gb
            else:
                grad[:, gcols] += gb
            return lg + dot_t(g_gate, bm[0, :, cols]) + dot_t(g_up, bm[1, :, cols])

        lg = lax.fori_loop(0, ff // FT, tile, jnp.zeros((nr, rank2), F32))
        lgb = (ADAPTER_SCALE * lg).astype(BF16)

        def gtile(i, carry):
            cols = ds(i, CT)
            ga = t_dot(lgb, xr[0, pl.ds(first, n), :, cols].reshape(nr, CT))
            if first == 0:
                grad[:, cols] = ga
            else:
                grad[:, cols] += ga
            return carry

        lax.fori_loop(0, width // CT, gtile, 0)

    def places(k):
        return (0,) if k == 0 else (7,) if k == NZ // 2 else (2 * k - 1, 2 * k)

    prepare(0)
    for h in (0, 1):
        relay(0, 0, h)
    loads[1].wait()
    for h in (0, 1):
        relay(1, 0, h)
    for a in (0, 1):
        for k in range(1, NZ // 2 + 1):
            for h in (0, 1):
                ring_copy(a, RIGHT, k, h).wait_recv()
                ring_copy(a, LEFT, k, h).wait_recv()
                if k < NZ // 2:
                    ring_start(a, k + 1, h)
                if a == 0 and k == NZ // 2 - 1 and h == 1:
                    ring_start(1, 1, 0)
                    ring_start(1, 1, 1)
                for p in places(k):
                    if a == 0 and h == 0:
                        metas[p].wait_recv()
                        prepare(p)
                    relay(a, p, h)
            if a == 0 and k == 1:
                for c in loads[2:]:
                    c.wait()
            if a == 0 and k >= 2:
                forward(k - 2)
            if a == 1 and k == 1:
                forward(3)
            if a == 1 and k == 2:
                backward(0, 1)
                backward(1, 2)
            if a == 1 and k == 3:
                backward(3, 2)

    groups = [(h, k) for k in range(NZ // 2, -1, -1) for h in (0, 1)]

    def ret_refs(h, p):
        return outs.at[p, :, half(h)], rets.at[p, :, half(h)], rt_s.at[h, p], rt_r.at[h, p]

    def ret_start(g):
        if g >= len(groups):
            return
        h, k = groups[g]
        for p in places(k):
            row_send(*ret_refs(h, p))

    GP = grad.shape[1] // 2
    NT = 2 * GP // 128
    WT = (NT + NZ - 1) // NZ

    def piece(q):
        return pl.ds(q * GP, GP)

    def dp_send(q):
        ysend[:, piece(q)] = grad[:, piece(q)].astype(BF16)
        for s in range(1, n_dp):
            to = lax.rem(dp + s, n_dp)
            copy_to(
                ysend.at[ds(to, part), piece(q)], yrecv.at[s - 1, :, piece(q)], y_s.at[0, q], y_r.at[0, q], dpdev(to)
            ).start()

    def tiles(q):
        return [(i % NZ, q * WT + i // NZ, i % 2, q * (NT // 2) + i // 2) for i in range(NT)]

    def owners(q):
        return pl.ds(q * WT, WT)

    def z_send(q):
        wait_bytes(yrecv.at[:, :, piece(q)], y_r.at[0, q])
        for zz, w, hh, c in tiles(q):
            cols = slice(c * 128, (c + 1) * 128)
            v = grad[pl.ds(pl.multiple_of(dp * part + hh * 16, 16), 16), cols]
            for s in range(n_dp - 1):
                v = v + yrecv[s, hh * 16 : (hh + 1) * 16, cols].astype(F32)
            t1[zz, w] = v.astype(BF16)
        for i in range(NT, WT * NZ):
            t1[i % NZ, q * WT + i // NZ] = jnp.zeros((16, 128), BF16)
        for s in range(1, NZ):
            to = lax.rem(z + s, NZ)
            copy_to(t1.at[to, owners(q)], r1.at[owners(q), z], g_s.at[0, q], g_r.at[0, q], zdev(s)).start()
        pltpu.make_async_copy(t1.at[z, owners(q)], r1.at[owners(q), z], g_r.at[0, q]).start()

    def row_copy(w):
        return copy_to(r1.at[w], r2.at[:, j], w_s.at[w], g_r.at[1, 0], rowdev(w))

    def x_send(q):
        wait_bytes(r1.at[owners(q)], g_r.at[0, q])
        for w in range(q * WT, (q + 1) * WT):

            @pl.when(j != w)
            def _(w=w):
                row_copy(w).start()

            @pl.when(j == w)
            def _(w=w):
                pltpu.make_async_copy(r1.at[w], r2.at[:, j], g_r.at[1, 0]).start()

    def owner(q):
        return (j >= q * WT) & (j < (q + 1) * WT)

    def x_sum(q):
        @pl.when(owner(q))
        def _():
            wait_bytes(r2, g_r.at[1, 0])
            pm = same[:, :slots].astype(BF16)
            r2f[...] = r2[...].reshape(slots * 16, 128).astype(F32)
            for t in range(16):
                rows = pl.ds(t, slots, stride=16)
                r2f[rows, :] = dot(pm, r2f[rows, :].astype(BF16))
            r2[...] = r2f[...].astype(BF16).reshape(NZ, ROW, 16, 128)
            for s in range(1, ROW):
                to = lax.rem(j + s, ROW)
                copy_to(r2.at[:, to], rb2.at[j], g_s.at[1, 0], g_r.at[2, q], rowdev(to)).start()
            pltpu.make_async_copy(r2.at[:, j], rb2.at[j], g_r.at[2, q]).start()

    def z_back(q):
        wait_bytes(rb2.at[owners(q)], g_r.at[2, q])
        for s in range(1, NZ):
            to = lax.rem(z + s, NZ)
            copy_to(rb2.at[owners(q), to], rb1.at[z, owners(q)], g_s.at[2, q], g_r.at[3, q], zdev(s)).start()
        pltpu.make_async_copy(rb2.at[owners(q), z], rb1.at[z, owners(q)], g_r.at[3, q]).start()

    def dp_back(q):
        wait_bytes(rb1.at[:, owners(q)], g_r.at[3, q])
        for zz, w, hh, c in tiles(q):
            yq[hh * 16 : (hh + 1) * 16, c * 128 : (c + 1) * 128] = rb1[zz, w]
        dst = yo.at[ds(dp, part), piece(q)]
        for s in range(1, n_dp):
            to = lax.rem(dp + s, n_dp)
            copy_to(yq.at[:, piece(q)], dst, y_s.at[1, q], y_r.at[1, q], dpdev(to)).start()
        pltpu.make_async_copy(yq.at[:, piece(q)], dst, y_r.at[1, q]).start()

    def turn(first, last):
        def block(i, carry):
            am[ds(i, BLK), :] = yo[:, ds(i, BLK)].astype(F32).T.astype(BF16)
            return carry

        lax.fori_loop(first, last, block, 0)

    def partial(h, p, store):
        _, dst, _, recv = ret_refs(h, p)
        wait_bytes(dst, recv)

        def tile(i, carry):
            cols = pl.ds(pl.multiple_of(h * HW + i * CT, CT), CT)
            r = rets[p, :, cols]
            store(cols, dot(whl[p, 0], r) + dot(whl[p, 1], r))
            return carry

        lax.fori_loop(0, HW // CT, tile, 0)

    def rs_copy(h, way, k):
        if k == 1:
            rows = pl.ds(0 if way == RIGHT else BLK // 2, BLK // 2)
            src, dst = xs.at[0, 7, rows, half(h)], rsr.at[way, 0, rows, half(h)]
        else:
            p = 2 * (NZ // 2 + 1 - k) - (0 if way == RIGHT else 1)
            src, dst = xs.at[0, p, :, half(h)], rsr.at[way, k - 1, :, half(h)]
        return copy_to(src, dst, rs_s.at[h, way, k - 1], rs_r.at[h, way, k - 1], zdev(1 if way == RIGHT else -1))

    def rs_step(h, k):
        if k == 1:

            def store(cols, v):
                xs[0, 7, :, cols] = v.astype(BF16)

            partial(h, 7, store)
            for way in (RIGHT, LEFT):
                rs_copy(h, way, 1).start()
            return
        for way in (RIGHT, LEFT):
            p = 2 * (NZ // 2 + 1 - k) - (0 if way == RIGHT else 1)
            rs_copy(h, way, k - 1).wait_recv()

            def store(cols, v, p=p, way=way):
                if k == 2:
                    m = BLK // 2
                    mine = slice(0, m) if way == RIGHT else slice(m, BLK)
                    rest = slice(m, BLK) if way == RIGHT else slice(0, m)
                    xs[0, p, mine, cols] = (v[mine] + rsr[way, 0, mine, cols].astype(F32)).astype(BF16)
                    xs[0, p, rest, cols] = v[rest].astype(BF16)
                else:
                    xs[0, p, :, cols] = (v + rsr[way, k - 2, :, cols].astype(F32)).astype(BF16)

            partial(h, p, store)
            rs_copy(h, way, k).start()

    def rs_last(h):
        for way in (RIGHT, LEFT):
            rs_copy(h, way, NZ // 2).wait_recv()
        src, _, send, _ = ret_refs(h, 0)
        row_sent(src, send)

        def store(cols, v):
            v = v + rsr[0, 3, :, cols].astype(F32) + rsr[1, 3, :, cols].astype(F32)
            outs[0, :, cols] = v.astype(BF16)

        partial(h, 0, store)
        c = pltpu.make_async_copy(outs.at[0, :, half(h)], mixed_out.at[:, half(h)], st.at[h])
        c.start()
        stores.append(c)

    stores = []

    def store_out(src, dst, i):
        c = pltpu.make_async_copy(src, dst, st.at[i])
        c.start()
        stores.append(c)

    rows_gone(1, 5)
    rows_gone(1, 6)
    ret_start(0)
    ret_start(1)
    backward(5, 2)
    rows_gone(1, 7)
    ret_start(2)
    backward(7, 1)
    dp_send(0)
    dp_send(1)
    rows_gone(0, 7)
    rs_step(0, 1)
    rs_step(1, 1)
    ret_start(3)
    z_send(0)
    rows_gone(0, 6)
    rows_gone(0, 5)
    rs_step(0, 2)
    z_send(1)
    x_send(0)
    ret_start(4)
    x_send(1)
    rs_step(1, 2)
    x_sum(0)
    ret_start(5)
    x_sum(1)
    rows_gone(0, 4)
    rows_gone(0, 3)
    rs_step(0, 3)
    ret_start(6)
    z_back(0)
    z_back(1)
    rs_step(1, 3)
    ret_start(7)
    dp_back(0)
    dp_back(1)
    rows_gone(0, 2)
    rows_gone(0, 1)
    rows_gone(0, 0)
    rs_step(0, 4)
    ret_start(8)
    ret_start(9)
    rs_step(1, 4)
    wait_bytes(yo.at[:, piece(0)], y_r.at[1, 0])
    turn(0, GP // BLK)
    wait_bytes(yo.at[:, piece(1)], y_r.at[1, 1])
    store_out(yo.at[:, pl.ds(width, ff)], grad_b_out, 3)
    turn(GP // BLK, width // BLK)
    store_out(am, grad_a_out, 2)
    rs_last(0)
    rs_last(1)

    for a in (0, 1):
        for k in range(1, NZ // 2 + 1):
            for h in (0, 1):
                ring_copy(a, RIGHT, k, h).wait_send()
                ring_copy(a, LEFT, k, h).wait_send()
    for c in metas.values():
        c.wait_send()
    for p in range(NZ):
        if p not in (5, 6, 7):
            rows_gone(1, p)
        for h in (0, 1):
            if p > 0:
                src, _, send, _ = ret_refs(h, p)
                row_sent(src, send)
    for h in (0, 1):
        for way in (RIGHT, LEFT):
            for k in range(1, NZ // 2 + 1):
                rs_copy(h, way, k).wait_send()
    for q in (0, 1):
        wait_bytes(yrecv.at[:, :, piece(q)], y_s.at[0, q])
        wait_bytes(yo.at[pl.ds(0, (n_dp - 1) * part), piece(q)], y_s.at[1, q])
        wait_bytes(rb1.at[pl.ds(0, NZ - 1), owners(q)], g_s.at[0, q])
        wait_bytes(rb1.at[pl.ds(0, NZ - 1), owners(q)], g_s.at[2, q])
        for w in range(q * WT, (q + 1) * WT):

            @pl.when(j != w)
            def _(w=w):
                row_copy(w).wait_send()

        @pl.when(owner(q))
        def _():
            wait_bytes(r1.at[pl.ds(0, ROW - 1)], g_s.at[1, 0])

    for c in stores:
        c.wait()


def body(tokens, cotangent, routing, weights, choice, table, gate_up, down, amap, bmap):
    n_dp = lax.axis_size("dp")
    tok, width = tokens.shape
    rank, ff = bmap.shape[2:]
    rank2 = 2 * rank
    gcols = width + ff
    part = rank2 // n_dp
    used = (2 * gcols // 128 + NZ - 1) // NZ
    hbm = pl.BlockSpec(memory_space=pl.ANY)
    vmem = pl.BlockSpec(memory_space=pltpu.VMEM)
    V = pltpu.VMEM
    S = pltpu.SemaphoreType.DMA
    mixed, grad_a, grad_b = pl.pallas_call(
        kernel,
        out_shape=(
            jax.ShapeDtypeStruct((tok, width), BF16),
            jax.ShapeDtypeStruct((width, rank2), BF16),
            jax.ShapeDtypeStruct((rank2, ff), BF16),
        ),
        in_specs=[hbm, hbm, vmem, vmem, vmem, vmem, hbm, hbm, hbm, hbm],
        out_specs=(hbm, hbm, hbm),
        scratch_shapes=[
            V((2, NZ, BLK, width), BF16),
            V((NZ, 2 * ROW, BLK), F32),
            V((NZ, 2 * ROW, BLK), F32),
            V((NZ, BLK, BLK), BF16),
            V((NZ, BLK, BLK), F32),
            V((NZ, 2, BLK, BLK), BF16),
            V((2, NZ, BLK, width), BF16),
            V((2, NZ, BLK, width), BF16),
            V((NZ, BLK, width), BF16),
            V((NZ, BLK, width), BF16),
            V((2, NZ // 2, BLK, width), BF16),
            V((width, 2 * ff), BF16),
            V((ff, width), BF16),
            V((width, rank2), BF16),
            V((2, rank2, ff), BF16),
            V((NZ * BLK, rank2), BF16),
            V((NZ * BLK, ff), F32),
            V((NZ * BLK, ff), F32),
            V((256, ff), BF16),
            V((rank2, gcols), F32),
            V((rank2, gcols), BF16),
            V((n_dp - 1, part, gcols), BF16),
            V((NZ, used, 16, 128), BF16),
            V((ROW, NZ, 16, 128), BF16),
            V((ROW, NZ, 16, 128), BF16),
            V((ROW * NZ * 16, 128), F32),
            V((ROW, NZ, 16, 128), BF16),
            V((NZ, used, 16, 128), BF16),
            V((part, gcols), BF16),
            V((rank2, gcols), BF16),
            S((7,)),
            S((2, 2, NZ // 2, 2)),
            S((2, 2, NZ // 2, 2)),
            S((NZ,)),
            S((NZ,)),
            S((2, NZ, 2)),
            S((2, NZ, 2)),
            S((2, NZ)),
            S((2, NZ)),
            S((2, 2, NZ // 2)),
            S((2, 2, NZ // 2)),
            S((2, 2)),
            S((2, 2)),
            S((3, 2)),
            S((4, 2)),
            S((used,)),
            S((4,)),
        ],
        compiler_params=pltpu.CompilerParams(
            collective_id=0, has_side_effects=True, vmem_limit_bytes=62 * 2**20
        ),
        cost_estimate=pl.CostEstimate(
            flops=16 * 10**9, bytes_accessed=14 * 2**20, transcendentals=NZ * BLK * ff
        ),
        name="moe_step",
    )(
        tokens, cotangent, routing.T, weights.T, choice.T, table.reshape(1, -1),
        gate_up[0], down[0], amap[0], bmap[0],
    )
    return mixed, grad_a.astype(F32)[None], grad_b.astype(F32).reshape(1, 2, rank, ff)


def solution(mesh):
    both = P(("dp", "expert"), None)
    return jax.shard_map(
        body,
        mesh=mesh,
        in_specs=(both, both, both, both, both, P(), P("expert", None, None), P("expert", None, None),
                  P("expert", None, None), P("expert", None, None, None)),
        out_specs=(both, P("expert", None, None), P("expert", None, None, None)),
        check_vma=False,
    )
```

```python
import jax
import jax.numpy as jnp
from jax import lax
from jax.experimental import pallas as pl
from jax.experimental.pallas import tpu as pltpu
from jax.sharding import PartitionSpec as P

ADAPTER_SCALE = 0.5
CAP = 16
ROW = 8
NZ = 8
BLK = 128
F32 = jnp.float32
BF16 = jnp.bfloat16
MESH = pl.DeviceIdType.MESH
RIGHT, LEFT = 0, 1


def dot(a, b):
    return jnp.dot(a, b, preferred_element_type=F32)


def dot_t(a, b):
    return lax.dot_general(a, b, (((1,), (1,)), ((), ())), preferred_element_type=F32)


def t_dot(a, b):
    return lax.dot_general(a, b, (((0,), (0,)), ((), ())), preferred_element_type=F32)


def ds(i, n):
    return pl.ds(pl.multiple_of(i * n, n), n)


def kernel(
    tokens, cots, routing, weights, choice, table, gate_up, down, amap, bmap,
    mixed_out, grad_a_out, grad_b_out,
    ring, meta, metar, pick, wcol, whl, xs, xr, outs, rets, rsr,
    gu, dn, am, bm, low, act, mul, hid, grad,
    ysend, yrecv, t1, r1, r2, r2f, rb2, rb1, yq, yo,
    ld, ag_s, ag_r, mt_s, mt_r, x_s, x_r, rt_s, rt_r, rs_s, rs_r, y_s, y_r, g_s, g_r, w_s, st,
):
    width = tokens.shape[1]
    ff = dn.shape[0]
    rank2 = am.shape[1]
    n_dp = yrecv.shape[0] + 1
    part = rank2 // n_dp
    dp = lax.axis_index("dp")
    e = lax.axis_index("expert")
    z, j = e // ROW, e % ROW

    def zdev(step):
        return (dp, lax.rem(z + step + NZ, NZ) * ROW + j)

    def rowdev(i):
        return (dp, z * ROW + i)

    def dpdev(i):
        return (i, e)

    bar = pltpu.get_barrier_semaphore()
    for s in range(1, NZ):
        pl.semaphore_signal(bar, inc=1, device_id=zdev(s), device_id_type=MESH)
    for s in range(1, ROW):
        pl.semaphore_signal(bar, inc=1, device_id=rowdev(lax.rem(j + s, ROW)), device_id_type=MESH)
    for s in range(1, n_dp):
        pl.semaphore_signal(bar, inc=1, device_id=dpdev(lax.rem(dp + s, n_dp)), device_id_type=MESH)

    rh = rank2 // 2
    loads = [
        pltpu.make_async_copy(tokens, ring.at[0, 0], ld.at[0]),
        pltpu.make_async_copy(cots, ring.at[1, 0], ld.at[1]),
        pltpu.make_async_copy(gate_up, gu, ld.at[2]),
        pltpu.make_async_copy(down, dn, ld.at[3]),
        pltpu.make_async_copy(amap, am, ld.at[4]),
        pltpu.make_async_copy(bmap.at[0], bm.at[0, pl.ds(0, rh)], ld.at[5]),
        pltpu.make_async_copy(bmap.at[1], bm.at[1, pl.ds(rh, rh)], ld.at[6]),
    ]
    for c in loads:
        c.start()
    bm[0, rh:, :] = jnp.zeros((rh, ff), BF16)
    bm[1, :rh, :] = jnp.zeros((rh, ff), BF16)

    slots = table.shape[1]
    top = routing.shape[0]
    trow = jnp.concatenate([table[...].astype(F32)] * (BLK // slots), axis=1)
    tcol = jnp.broadcast_to(trow, (BLK, BLK)).T[:slots]
    same = (tcol == trow).astype(F32)
    sub = lax.broadcasted_iota(jnp.int32, (slots, BLK), 0)
    lane = lax.broadcasted_iota(jnp.int32, (slots, BLK), 1)
    cnt = jnp.sum(jnp.where(lane < slots, same, 0.0), axis=1, keepdims=True)
    occ = jnp.sum(jnp.where(lane < sub, same, 0.0), axis=1, keepdims=True)
    picked = jnp.zeros((slots, BLK), F32)
    wsum = jnp.zeros((slots, BLK), F32)
    for k in range(top):
        want = choice[k : k + 1, :].astype(F32)
        want = want - cnt * jnp.floor((want + 0.5) / cnt)
        hit = (tcol == routing[k : k + 1, :].astype(F32)) & (want == occ)
        picked = jnp.where(hit, 1.0, picked)
        wsum = jnp.where(hit, weights[k : k + 1, :], wsum)
    tri = lax.broadcasted_iota(jnp.int32, (BLK, BLK), 0) < lax.broadcasted_iota(jnp.int32, (BLK, BLK), 1)
    ahead = dot(picked.astype(BF16), tri.astype(F32).astype(BF16))
    rank = jnp.where(picked > 0.0, ahead, -1.0)
    for i in range(NZ):
        meta[i, :ROW] = rank[i * ROW : (i + 1) * ROW]
        meta[i, ROW:] = wsum[i * ROW : (i + 1) * ROW]
    metar[0] = meta[z]
    pl.semaphore_wait(bar, NZ - 1 + ROW - 1 + n_dp - 1)

    def copy_to(src, dst, send, recv, device):
        return pltpu.make_async_remote_copy(
            src_ref=src, dst_ref=dst, send_sem=send, recv_sem=recv, device_id=device, device_id_type=MESH
        )

    def wait_bytes(ref, sem):
        pltpu.make_async_copy(ref, ref, sem).wait()

    HW = width // 2

    def half(h):
        return pl.ds(h * HW, HW)

    def ring_copy(a, way, k, h):
        if way == RIGHT:
            frm, to, dev = (0 if k == 1 else 2 * k - 3), 2 * k - 1, zdev(1)
        else:
            frm, to, dev = 2 * k - 2, min(2 * k, NZ - 1), zdev(-1)
        rows = pl.ds(0, BLK)
        if k == NZ // 2:
            rows = pl.ds(0 if way == RIGHT else BLK // 2, BLK // 2)
        src, dst = ring.at[a, frm, rows, half(h)], ring.at[a, to, rows, half(h)]
        return copy_to(src, dst, ag_s.at[a, way, k - 1, h], ag_r.at[a, way, k - 1, h], dev)

    def ring_start(a, k, h):
        ring_copy(a, RIGHT, k, h).start()
        ring_copy(a, LEFT, k, h).start()

    loads[0].wait()
    ring_start(0, 1, 0)
    ring_start(0, 1, 1)

    def meta_copy(s):
        place = 2 * s - 1 if s <= NZ // 2 else 2 * (NZ - s)
        dst_row = lax.rem(z + s, NZ)
        return place, copy_to(meta.at[dst_row], metar.at[place], mt_s.at[place], mt_r.at[place], zdev(s))

    metas = dict(meta_copy(s) for s in range(1, NZ))
    for c in metas.values():
        c.start()

    def prepare(p):
        order = lax.broadcasted_iota(jnp.int32, (CAP, BLK), 0).astype(F32)
        parts = []
        for i in range(ROW):
            rows = slice(i * CAP, (i + 1) * CAP)
            hit = jnp.broadcast_to(metar[p, i : i + 1, :], (CAP, BLK)) == order
            pick[p, rows] = jnp.where(hit, 1.0, 0.0).astype(BF16)
            w = jnp.where(hit, jnp.broadcast_to(metar[p, ROW + i : ROW + i + 1, :], (CAP, BLK)), 0.0)
            wcol[p, rows] = jnp.broadcast_to(jnp.sum(w, axis=1, keepdims=True), (CAP, BLK))
            parts.append(w)
        wt = jnp.concatenate(parts, axis=0).T
        hi = wt.astype(BF16)
        whl[p, 0] = hi
        whl[p, 1] = (wt - hi.astype(F32)).astype(BF16)

    CT = 512

    def relay(a, p, h):
        def tile(i, carry):
            cols = pl.ds(pl.multiple_of(h * HW + i * CT, CT), CT)
            v = dot(pick[p], ring[a, p, :, cols])
            if a == 1:
                v = v * wcol[p][:, 0:1]
            xs[a, p, :, cols] = v.astype(BF16)
            return carry

        lax.fori_loop(0, HW // CT, tile, 0)
        row_send(xs.at[a, p, :, half(h)], xr.at[a, p, :, half(h)], x_s.at[a, p, h], x_r.at[a, p, h])

    def rows_here(a, p):
        for h in (0, 1):
            wait_bytes(xr.at[a, p, :, half(h)], x_r.at[a, p, h])

    def rows_gone(a, p):
        for h in (0, 1):
            row_sent(xs.at[a, p, :, half(h)], x_s.at[a, p, h])

    def row_send(src, dst, send, recv):
        mine = ds(j, CAP)
        for s in range(1, ROW):
            to = lax.rem(j + s, ROW)
            copy_to(src.at[ds(to, CAP)], dst.at[mine], send, recv, rowdev(to)).start()
        pltpu.make_async_copy(src.at[mine], dst.at[mine], recv).start()

    def row_sent(src, send):
        wait_bytes(src.at[pl.ds(0, (ROW - 1) * CAP)], send)

    FT = 256
    CH = 256

    def forward(c):
        for p in (2 * c, 2 * c + 1):
            rows_here(0, p)
        rows = pl.ds(c * CH, CH)
        x = xr.at[0, pl.ds(2 * c, 2)]

        def xv():
            return x[...].reshape(CH, width)

        low[rows, :] = dot(xv(), am[...]).astype(BF16)

        def tile(f, carry):
            cols = ds(f, FT)
            up_cols = pl.ds(pl.multiple_of(ff + f * FT, FT), FT)
            lw = low[rows, :]
            pg = dot(xv(), gu[:, cols]) + ADAPTER_SCALE * dot(lw, bm[0, :, cols])
            pu = dot(xv(), gu[:, up_cols]) + ADAPTER_SCALE * dot(lw, bm[1, :, cols])
            sig = jax.nn.sigmoid(pg)
            ac = pg * sig
            act[rows, cols] = ac
            mul[rows, cols] = pu * (sig * (1.0 + pg * (1.0 - sig)))
            hid[:, cols] = (ac * pu).astype(BF16)
            return carry

        lax.fori_loop(0, ff // FT, tile, 0)

        def otile(i, carry):
            cols = ds(i, CT)
            o = dot(hid[...], dn[:, cols]).astype(BF16)
            outs[2 * c, :, cols] = o[:BLK]
            outs[2 * c + 1, :, cols] = o[BLK:]
            return carry

        lax.fori_loop(0, width // CT, otile, 0)

    def backward(first, n):
        for p in range(first, first + n):
            rows_here(1, p)
        nr = n * BLK
        rows = pl.ds(first * BLK, nr)

        def tile(f, lg):
            cols = ds(f, FT)
            gcols = pl.ds(pl.multiple_of(width + f * FT, FT), FT)
            back = dot_t(xr[1, pl.ds(first, n)].reshape(nr, width), dn[cols, :])
            g_up = (back * act[rows, cols]).astype(BF16)
            g_gate = (back * mul[rows, cols]).astype(BF16)
            lw = low[rows, :]
            gb0 = ADAPTER_SCALE * t_dot(lw, g_gate)
            gb1 = ADAPTER_SCALE * t_dot(lw, g_up)
            gb = jnp.concatenate([gb0[:rh], gb1[rh:]], axis=0)
            if first == 0:
                grad[:, gcols] = gb
            else:
                grad[:, gcols] += gb
            return lg + dot_t(g_gate, bm[0, :, cols]) + dot_t(g_up, bm[1, :, cols])

        lg = lax.fori_loop(0, ff // FT, tile, jnp.zeros((nr, rank2), F32))
        lgb = (ADAPTER_SCALE * lg).astype(BF16)

        def gtile(i, carry):
            cols = ds(i, CT)
            ga = t_dot(lgb, xr[0, pl.ds(first, n), :, cols].reshape(nr, CT))
            if first == 0:
                grad[:, cols] = ga
            else:
                grad[:, cols] += ga
            return carry

        lax.fori_loop(0, width // CT, gtile, 0)

    def places(k):
        return (0,) if k == 0 else (7,) if k == NZ // 2 else (2 * k - 1, 2 * k)

    prepare(0)
    for h in (0, 1):
        relay(0, 0, h)
    loads[1].wait()
    for h in (0, 1):
        relay(1, 0, h)
    for a in (0, 1):
        for k in range(1, NZ // 2 + 1):
            for h in (0, 1):
                ring_copy(a, RIGHT, k, h).wait_recv()
                ring_copy(a, LEFT, k, h).wait_recv()
                if k < NZ // 2:
                    ring_start(a, k + 1, h)
                if a == 0 and k == NZ // 2 - 1 and h == 1:
                    ring_start(1, 1, 0)
                    ring_start(1, 1, 1)
                for p in places(k):
                    if a == 0 and h == 0:
                        metas[p].wait_recv()
                        prepare(p)
                    relay(a, p, h)
            if a == 0 and k == 1:
                for c in loads[2:]:
                    c.wait()
            if a == 0 and k >= 2:
                forward(k - 2)
            if a == 1 and k == 1:
                forward(3)
            if a == 1 and k == 2:
                backward(0, 1)
                backward(1, 2)
            if a == 1 and k == 3:
                backward(3, 2)

    groups = [(h, k) for k in range(NZ // 2, -1, -1) for h in (0, 1)]

    def ret_refs(h, p):
        return outs.at[p, :, half(h)], rets.at[p, :, half(h)], rt_s.at[h, p], rt_r.at[h, p]

    def ret_start(g):
        if g >= len(groups):
            return
        h, k = groups[g]
        for p in places(k):
            row_send(*ret_refs(h, p))

    GP = grad.shape[1] // 2
    NT = 2 * GP // 128
    WT = (NT + NZ - 1) // NZ

    def piece(q):
        return pl.ds(q * GP, GP)

    def dp_send(q):
        ysend[:, piece(q)] = grad[:, piece(q)].astype(BF16)
        for s in range(1, n_dp):
            to = lax.rem(dp + s, n_dp)
            copy_to(
                ysend.at[ds(to, part), piece(q)], yrecv.at[s - 1, :, piece(q)], y_s.at[0, q], y_r.at[0, q], dpdev(to)
            ).start()

    def tiles(q):
        return [(i % NZ, q * WT + i // NZ, i % 2, q * (NT // 2) + i // 2) for i in range(NT)]

    def owners(q):
        return pl.ds(q * WT, WT)

    def z_send(q):
        wait_bytes(yrecv.at[:, :, piece(q)], y_r.at[0, q])
        for zz, w, hh, c in tiles(q):
            cols = slice(c * 128, (c + 1) * 128)
            v = grad[pl.ds(pl.multiple_of(dp * part + hh * 16, 16), 16), cols]
            for s in range(n_dp - 1):
                v = v + yrecv[s, hh * 16 : (hh + 1) * 16, cols].astype(F32)
            t1[zz, w] = v.astype(BF16)
        for i in range(NT, WT * NZ):
            t1[i % NZ, q * WT + i // NZ] = jnp.zeros((16, 128), BF16)
        for s in range(1, NZ):
            to = lax.rem(z + s, NZ)
            copy_to(t1.at[to, owners(q)], r1.at[owners(q), z], g_s.at[0, q], g_r.at[0, q], zdev(s)).start()
        pltpu.make_async_copy(t1.at[z, owners(q)], r1.at[owners(q), z], g_r.at[0, q]).start()

    def row_copy(w):
        return copy_to(r1.at[w], r2.at[:, j], w_s.at[w], g_r.at[1, 0], rowdev(w))

    def x_send(q):
        wait_bytes(r1.at[owners(q)], g_r.at[0, q])
        for w in range(q * WT, (q + 1) * WT):

            @pl.when(j != w)
            def _(w=w):
                row_copy(w).start()

            @pl.when(j == w)
            def _(w=w):
                pltpu.make_async_copy(r1.at[w], r2.at[:, j], g_r.at[1, 0]).start()

    def owner(q):
        return (j >= q * WT) & (j < (q + 1) * WT)

    def x_sum(q):
        @pl.when(owner(q))
        def _():
            wait_bytes(r2, g_r.at[1, 0])
            pm = same[:, :slots].astype(BF16)
            r2f[...] = r2[...].reshape(slots * 16, 128).astype(F32)
            for t in range(16):
                rows = pl.ds(t, slots, stride=16)
                r2f[rows, :] = dot(pm, r2f[rows, :].astype(BF16))
            r2[...] = r2f[...].astype(BF16).reshape(NZ, ROW, 16, 128)
            for s in range(1, ROW):
                to = lax.rem(j + s, ROW)
                copy_to(r2.at[:, to], rb2.at[j], g_s.at[1, 0], g_r.at[2, q], rowdev(to)).start()
            pltpu.make_async_copy(r2.at[:, j], rb2.at[j], g_r.at[2, q]).start()

    def z_back(q):
        wait_bytes(rb2.at[owners(q)], g_r.at[2, q])
        for s in range(1, NZ):
            to = lax.rem(z + s, NZ)
            copy_to(rb2.at[owners(q), to], rb1.at[z, owners(q)], g_s.at[2, q], g_r.at[3, q], zdev(s)).start()
        pltpu.make_async_copy(rb2.at[owners(q), z], rb1.at[z, owners(q)], g_r.at[3, q]).start()

    def dp_back(q):
        wait_bytes(rb1.at[:, owners(q)], g_r.at[3, q])
        for zz, w, hh, c in tiles(q):
            yq[hh * 16 : (hh + 1) * 16, c * 128 : (c + 1) * 128] = rb1[zz, w]
        dst = yo.at[ds(dp, part), piece(q)]
        for s in range(1, n_dp):
            to = lax.rem(dp + s, n_dp)
            copy_to(yq.at[:, piece(q)], dst, y_s.at[1, q], y_r.at[1, q], dpdev(to)).start()
        pltpu.make_async_copy(yq.at[:, piece(q)], dst, y_r.at[1, q]).start()

    def turn(first, last):
        def block(i, carry):
            am[ds(i, BLK), :] = yo[:, ds(i, BLK)].astype(F32).T.astype(BF16)
            return carry

        lax.fori_loop(first, last, block, 0)

    def partial(h, p, store):
        _, dst, _, recv = ret_refs(h, p)
        wait_bytes(dst, recv)

        def tile(i, carry):
            cols = pl.ds(pl.multiple_of(h * HW + i * CT, CT), CT)
            r = rets[p, :, cols]
            store(cols, dot(whl[p, 0], r) + dot(whl[p, 1], r))
            return carry

        lax.fori_loop(0, HW // CT, tile, 0)

    def rs_copy(h, way, k):
        if k == 1:
            rows = pl.ds(0 if way == RIGHT else BLK // 2, BLK // 2)
            src, dst = xs.at[0, 7, rows, half(h)], rsr.at[way, 0, rows, half(h)]
        else:
            p = 2 * (NZ // 2 + 1 - k) - (0 if way == RIGHT else 1)
            src, dst = xs.at[0, p, :, half(h)], rsr.at[way, k - 1, :, half(h)]
        return copy_to(src, dst, rs_s.at[h, way, k - 1], rs_r.at[h, way, k - 1], zdev(1 if way == RIGHT else -1))

    def rs_step(h, k):
        if k == 1:

            def store(cols, v):
                xs[0, 7, :, cols] = v.astype(BF16)

            partial(h, 7, store)
            for way in (RIGHT, LEFT):
                rs_copy(h, way, 1).start()
            return
        for way in (RIGHT, LEFT):
            p = 2 * (NZ // 2 + 1 - k) - (0 if way == RIGHT else 1)
            rs_copy(h, way, k - 1).wait_recv()

            def store(cols, v, p=p, way=way):
                if k == 2:
                    m = BLK // 2
                    mine = slice(0, m) if way == RIGHT else slice(m, BLK)
                    rest = slice(m, BLK) if way == RIGHT else slice(0, m)
                    xs[0, p, mine, cols] = (v[mine] + rsr[way, 0, mine, cols].astype(F32)).astype(BF16)
                    xs[0, p, rest, cols] = v[rest].astype(BF16)
                else:
                    xs[0, p, :, cols] = (v + rsr[way, k - 2, :, cols].astype(F32)).astype(BF16)

            partial(h, p, store)
            rs_copy(h, way, k).start()

    def rs_last(h):
        for way in (RIGHT, LEFT):
            rs_copy(h, way, NZ // 2).wait_recv()
        src, _, send, _ = ret_refs(h, 0)
        row_sent(src, send)

        def store(cols, v):
            v = v + rsr[0, 3, :, cols].astype(F32) + rsr[1, 3, :, cols].astype(F32)
            outs[0, :, cols] = v.astype(BF16)

        partial(h, 0, store)
        c = pltpu.make_async_copy(outs.at[0, :, half(h)], mixed_out.at[:, half(h)], st.at[h])
        c.start()
        stores.append(c)

    stores = []

    def store_out(src, dst, i):
        c = pltpu.make_async_copy(src, dst, st.at[i])
        c.start()
        stores.append(c)

    rows_gone(1, 5)
    rows_gone(1, 6)
    ret_start(0)
    ret_start(1)
    backward(5, 2)
    rows_gone(1, 7)
    ret_start(2)
    backward(7, 1)
    dp_send(0)
    dp_send(1)
    rows_gone(0, 7)
    rs_step(0, 1)
    rs_step(1, 1)
    ret_start(3)
    z_send(0)
    rows_gone(0, 6)
    rows_gone(0, 5)
    rs_step(0, 2)
    z_send(1)
    x_send(0)
    ret_start(4)
    x_send(1)
    rs_step(1, 2)
    x_sum(0)
    ret_start(5)
    x_sum(1)
    ret_start(6)
    rows_gone(0, 4)
    rows_gone(0, 3)
    rs_step(0, 3)
    ret_start(7)
    z_back(0)
    z_back(1)
    ret_start(8)
    rs_step(1, 3)
    ret_start(9)
    dp_back(0)
    dp_back(1)
    rows_gone(0, 2)
    rows_gone(0, 1)
    rows_gone(0, 0)
    rs_step(0, 4)
    rs_step(1, 4)
    wait_bytes(yo.at[:, piece(0)], y_r.at[1, 0])
    turn(0, GP // BLK)
    wait_bytes(yo.at[:, piece(1)], y_r.at[1, 1])
    store_out(yo.at[:, pl.ds(width, ff)], grad_b_out, 3)
    turn(GP // BLK, width // BLK)
    store_out(am, grad_a_out, 2)
    rs_last(0)
    rs_last(1)

    for a in (0, 1):
        for k in range(1, NZ // 2 + 1):
            for h in (0, 1):
                ring_copy(a, RIGHT, k, h).wait_send()
                ring_copy(a, LEFT, k, h).wait_send()
    for c in metas.values():
        c.wait_send()
    for p in range(NZ):
        if p not in (5, 6, 7):
            rows_gone(1, p)
        for h in (0, 1):
            if p > 0:
                src, _, send, _ = ret_refs(h, p)
                row_sent(src, send)
    for h in (0, 1):
        for way in (RIGHT, LEFT):
            for k in range(1, NZ // 2 + 1):
                rs_copy(h, way, k).wait_send()
    for q in (0, 1):
        wait_bytes(yrecv.at[:, :, piece(q)], y_s.at[0, q])
        wait_bytes(yo.at[pl.ds(0, (n_dp - 1) * part), piece(q)], y_s.at[1, q])
        wait_bytes(rb1.at[pl.ds(0, NZ - 1), owners(q)], g_s.at[0, q])
        wait_bytes(rb1.at[pl.ds(0, NZ - 1), owners(q)], g_s.at[2, q])
        for w in range(q * WT, (q + 1) * WT):

            @pl.when(j != w)
            def _(w=w):
                row_copy(w).wait_send()

        @pl.when(owner(q))
        def _():
            wait_bytes(r1.at[pl.ds(0, ROW - 1)], g_s.at[1, 0])

    for c in stores:
        c.wait()


def body(tokens, cotangent, routing, weights, choice, table, gate_up, down, amap, bmap):
    n_dp = lax.axis_size("dp")
    tok, width = tokens.shape
    rank, ff = bmap.shape[2:]
    rank2 = 2 * rank
    gcols = width + ff
    part = rank2 // n_dp
    used = (2 * gcols // 128 + NZ - 1) // NZ
    hbm = pl.BlockSpec(memory_space=pl.ANY)
    vmem = pl.BlockSpec(memory_space=pltpu.VMEM)
    V = pltpu.VMEM
    S = pltpu.SemaphoreType.DMA
    mixed, grad_a, grad_b = pl.pallas_call(
        kernel,
        out_shape=(
            jax.ShapeDtypeStruct((tok, width), BF16),
            jax.ShapeDtypeStruct((width, rank2), BF16),
            jax.ShapeDtypeStruct((rank2, ff), BF16),
        ),
        in_specs=[hbm, hbm, vmem, vmem, vmem, vmem, hbm, hbm, hbm, hbm],
        out_specs=(hbm, hbm, hbm),
        scratch_shapes=[
            V((2, NZ, BLK, width), BF16),
            V((NZ, 2 * ROW, BLK), F32),
            V((NZ, 2 * ROW, BLK), F32),
            V((NZ, BLK, BLK), BF16),
            V((NZ, BLK, BLK), F32),
            V((NZ, 2, BLK, BLK), BF16),
            V((2, NZ, BLK, width), BF16),
            V((2, NZ, BLK, width), BF16),
            V((NZ, BLK, width), BF16),
            V((NZ, BLK, width), BF16),
            V((2, NZ // 2, BLK, width), BF16),
            V((width, 2 * ff), BF16),
            V((ff, width), BF16),
            V((width, rank2), BF16),
            V((2, rank2, ff), BF16),
            V((NZ * BLK, rank2), BF16),
            V((NZ * BLK, ff), F32),
            V((NZ * BLK, ff), F32),
            V((256, ff), BF16),
            V((rank2, gcols), F32),
            V((rank2, gcols), BF16),
            V((n_dp - 1, part, gcols), BF16),
            V((NZ, used, 16, 128), BF16),
            V((ROW, NZ, 16, 128), BF16),
            V((ROW, NZ, 16, 128), BF16),
            V((ROW * NZ * 16, 128), F32),
            V((ROW, NZ, 16, 128), BF16),
            V((NZ, used, 16, 128), BF16),
            V((part, gcols), BF16),
            V((rank2, gcols), BF16),
            S((7,)),
            S((2, 2, NZ // 2, 2)),
            S((2, 2, NZ // 2, 2)),
            S((NZ,)),
            S((NZ,)),
            S((2, NZ, 2)),
            S((2, NZ, 2)),
            S((2, NZ)),
            S((2, NZ)),
            S((2, 2, NZ // 2)),
            S((2, 2, NZ // 2)),
            S((2, 2)),
            S((2, 2)),
            S((3, 2)),
            S((4, 2)),
            S((used,)),
            S((4,)),
        ],
        compiler_params=pltpu.CompilerParams(
            collective_id=0, has_side_effects=True, vmem_limit_bytes=62 * 2**20
        ),
        cost_estimate=pl.CostEstimate(
            flops=16 * 10**9, bytes_accessed=14 * 2**20, transcendentals=NZ * BLK * ff
        ),
        name="moe_step",
    )(
        tokens, cotangent, routing.T, weights.T, choice.T, table.reshape(1, -1),
        gate_up[0], down[0], amap[0], bmap[0],
    )
    return mixed, grad_a.astype(F32)[None], grad_b.astype(F32).reshape(1, 2, rank, ff)


def solution(mesh):
    both = P(("dp", "expert"), None)
    return jax.shard_map(
        body,
        mesh=mesh,
        in_specs=(both, both, both, both, both, P(), P("expert", None, None), P("expert", None, None),
                  P("expert", None, None), P("expert", None, None, None)),
        out_specs=(both, P("expert", None, None), P("expert", None, None, None)),
        check_vma=False,
    )
```
